32 devices in a mesh: gen: 4 (over y, core), voc: 8 (over z, x).
Axes of the slice: x: 2, y: 2, z: 4, core: 2. Of those that a mesh axis runs over, the one named last changes fastest.
Arguments:
- features: bfloat16 [2048, 24, 128], P(('gen', 'voc')), may hold values from -6 to 6
- target: int32 [2048], P(('gen', 'voc')), may hold values from -1 to 255, as said below
- extents: int32 [2048, 3], P(('gen', 'voc')), may hold values from 0 to 24, as said below
- w_pre: bfloat16 [896, 1536], replicated, may hold values from -0.1875 to 0.1875
- biases: float32 [1536], replicated, may hold values from -1.5 to 1.5
- snake_params: float32 [2, 1536], replicated, may hold values from 0.4 to 2.5
- w_up: bfloat16 [1536, 6144], replicated, may hold values from -0.109375 to 0.109375
- up_bias: float32 [768], replicated, may hold values from -1.5 to 1.5
Outputs:
- waves: bfloat16 [2048, 96, 768], P(('gen', 'voc'))
The draws below stay inside these ranges and needn't reach their ends.
Inputs may be any that keep to these rules, and one draw needn't show every extreme that they name: Within each gen group every (voc index, slot) pair target[i] = voc index * 32 + slot is named by exactly one generator slot; -1 marks an empty generator slot. No generator device names one vocoder device more than 8 times, and in every group some device does so exactly 8 times for each vocoder device. `extents`: column 0 is 24 except for the last segment of an utterance; columns 1 and 2 are 0 where the stream neighbour belongs to another utterance and equal its column 0 otherwise; all zero for empty slots.
All inputs are finite; a program needn't handle non-finite values.
Results may differ from the reference program's by a relative error of at most 0.0048.
Values may be sent and summed in bfloat16 or wider, within the bound.
A program may use at most 192 MiB of HBM per device.

```python
import math
import jax
import jax.numpy as jnp
from jax import lax

FEAT = 128
CH = 1536
CH2 = 768
UP = 4
KPRE = 7
SEG = 24
SLOT = 32
RIM = 4
SRC_CAP = 64
CAP = 8
SOURCE_SLOTS = 2048
N_GEN = 4
N_VOC = 8


def stream_plan(key):
    device_count = N_GEN * N_VOC
    stream_len = SLOT * device_count
    key_start, key_last, key_extra, key_sign, key_force = jax.random.split(key, 5)
    cells = jnp.arange(stream_len, dtype=jnp.int32)
    starts = jax.random.randint(key_start, (stream_len,), 0, 5) == 0
    starts = starts | (cells == 0) | (cells == stream_len // 2)
    is_last = jnp.roll(starts, -1)
    last_len = jax.random.randint(key_last, (stream_len,), 1, SEG + 1)
    seg_frames = jnp.where(is_last, last_len, SEG).astype(jnp.int32)
    prev_frames = jnp.where(starts, 0, jnp.roll(seg_frames, 1)).astype(jnp.int32)
    next_frames = jnp.where(is_last, 0, jnp.roll(seg_frames, -1)).astype(jnp.int32)
    half_cap = CAP // 2
    pair_count = N_VOC // 2
    extra = jax.random.randint(key_extra, (N_GEN, N_VOC, pair_count), 0, half_cap + 1)
    forced = jax.random.randint(key_force, (N_GEN, N_VOC), 0, pair_count)
    extra = jnp.where(jnp.arange(pair_count)[None, None, :] == forced[:, :, None], half_cap, extra)
    signs = jax.random.randint(key_sign, (N_GEN, N_VOC, pair_count), 0, 2) * 2 - 1
    counts = jnp.stack([half_cap + signs * extra, half_cap - signs * extra], axis=-1)
    counts = jnp.transpose(counts.reshape(N_GEN, N_VOC, N_VOC), (0, 2, 1)).astype(jnp.int32)
    row_start = jnp.cumsum(counts, axis=2) - counts
    col_start = jnp.cumsum(counts, axis=1) - counts
    slot_ids = jnp.arange(SRC_CAP, dtype=jnp.int32)[None, None, None, :]
    inside = (slot_ids >= row_start[..., None]) & (slot_ids < row_start[..., None] + counts[..., None])
    stream_slot = col_start[..., None] + slot_ids - row_start[..., None]
    worker_ids = jnp.arange(N_VOC, dtype=jnp.int32)[None, None, :, None]
    group_ids = jnp.arange(N_GEN, dtype=jnp.int32)[:, None, None, None]
    codes = worker_ids * SLOT + stream_slot
    places = stream_slot * device_count + group_ids * N_VOC + worker_ids
    used = jnp.any(inside, axis=2)
    target = jnp.where(used, jnp.sum(jnp.where(inside, codes, 0), axis=2), -1)
    position = jnp.where(used, jnp.sum(jnp.where(inside, places, 0), axis=2), 0)
    table = jnp.stack([seg_frames, prev_frames, next_frames], axis=1)
    extents = jnp.where(used[..., None], table[position], 0)
    return (target.reshape(-1).astype(jnp.int32), extents.reshape(-1, 3).astype(jnp.int32))


def draw_target(key, part):
    return stream_plan(key)[0]


def draw_extents(key, part):
    return stream_plan(key)[1]


def level_of(own_key, dims, cuts, smallest, largest):
    level, own = 1.0, jax.random.fold_in(own_key, 6)
    for axis_at, parts in cuts:
        heights = jnp.exp(jax.random.uniform(jax.random.fold_in(own, axis_at), (parts,), jnp.float32, smallest / len(cuts), largest / len(cuts)))
        level = level * jnp.repeat(heights, dims[axis_at] // parts).reshape([-1 if axis == axis_at else 1 for axis in range(len(dims))])
    return level


def gaussian(own_key, extent, deviation, bound, cuts=(), kind=jnp.bfloat16):
    values = deviation * jax.random.normal(own_key, extent, jnp.float32)
    if cuts:
        values = values * level_of(own_key, extent, cuts, -0.22, 0.18)
    return jnp.clip(values, -bound, bound).astype(kind)


def setup_inputs(seed: int = 0) -> dict:
    seeds = jax.random.split(jax.random.key(seed), 9)
    features = gaussian(seeds[0], (SOURCE_SLOTS, SEG, FEAT), 1.0, 6.0, ((0, 32),))
    target = draw_target(jax.random.fold_in(seeds[8], 71), 0)
    extents = draw_extents(jax.random.fold_in(seeds[8], 71), 0)
    w_pre = gaussian(seeds[3], (KPRE * FEAT, CH), (KPRE * FEAT) ** -0.5, 0.1875)
    biases = gaussian(seeds[4], (CH,), 0.3, 1.5, (), jnp.float32)
    snake_params = jnp.clip(jnp.exp(jax.random.uniform(seeds[5], (2, CH), jnp.float32, math.log(0.4), math.log(2.5))), 0.4, 2.5)
    w_up = gaussian(seeds[6], (CH, 2 * UP * CH2), (2 * CH) ** -0.5, 0.109375)
    up_bias = gaussian(seeds[7], (CH2,), 0.3, 1.5, (), jnp.float32)
    return dict(features=features, target=target, extents=extents, w_pre=w_pre, biases=biases, snake_params=snake_params, w_up=w_up, up_bias=up_bias)


def stacked_taps(values, kernel):
    length = values.shape[1] - (kernel - 1)
    pieces = [values[:, tap_index: tap_index + length] for tap_index in range(kernel)]
    return jnp.concatenate(pieces, axis=2)


def convolve(values, weight, kernel):
    stacked = stacked_taps(values, kernel)
    flattened = stacked.reshape(-1, stacked.shape[2])
    result = jnp.dot(flattened, weight, preferred_element_type=jnp.float32)
    return result.reshape(stacked.shape[0], stacked.shape[1], weight.shape[1])


def snake_act(values, alpha, beta):
    return values + jnp.square(jnp.sin(alpha * values)) / beta


def window_mask(extent_rows, seg_len):
    rim_cells = jnp.arange(RIM, dtype=jnp.int32)
    cells = jnp.arange(seg_len, dtype=jnp.int32)
    before = rim_cells[None, :] + seg_len - RIM < extent_rows[:, 1:2]
    own_part = cells[None, :] < extent_rows[:, 0:1]
    after = rim_cells[None, :] < extent_rows[:, 2:3]
    return jnp.concatenate([before, own_part, after], axis=1).astype(jnp.float32)


def trunk(window, frame_mask, w_pre, biases, snake_params):
    first = (KPRE - 1) // 2
    span = window.shape[1]
    inputs = window * frame_mask[:, :, None].astype(jnp.bfloat16)
    hidden = frame_mask[:, first:span - first, None] * (convolve(inputs, w_pre, KPRE) + biases)
    return snake_act(hidden, snake_params[0], snake_params[1]).astype(jnp.bfloat16)


def upsample(activations, seg_mask, w_up, up_bias):
    projected = jnp.dot(activations.reshape(-1, activations.shape[2]), w_up, preferred_element_type=jnp.float32)
    projected = projected.reshape(activations.shape[0], activations.shape[1], 2 * UP, up_bias.shape[0])
    centre = projected[:, 1:-1, UP // 2: UP // 2 + UP]
    side = jnp.concatenate([projected[:, :-2, 3 * UP // 2:], projected[:, 2:, :UP // 2]], axis=2)
    samples = seg_mask[:, :, None, None] * (centre + side + up_bias)
    return samples.astype(jnp.bfloat16).reshape(activations.shape[0], -1, up_bias.shape[0])


def reference(features, target, extents, w_pre, biases, snake_params, w_up, up_bias):
    device_count = N_GEN * N_VOC
    stream_len = SLOT * device_count
    source_ids = jnp.arange(SOURCE_SLOTS, dtype=jnp.int32)
    group_index = source_ids // (SRC_CAP * N_VOC)
    worker = group_index * N_VOC + target // SLOT
    position = jnp.where(target >= 0, (target % SLOT) * device_count + worker, stream_len).astype(jnp.int32)
    stream_feat = jnp.zeros((stream_len, SEG, FEAT), jnp.bfloat16).at[position].set(features, mode="drop")
    stream_ext = jnp.zeros((stream_len, 3), jnp.int32).at[position].set(extents, mode="drop")
    windows = jnp.concatenate([jnp.roll(stream_feat, 1, axis=0)[:, SEG - RIM:], stream_feat,
                               jnp.roll(stream_feat, -1, axis=0)[:, :RIM]], axis=1)
    window_masks = window_mask(stream_ext, SEG)

    def vocode(block_pair):
        window_block, mask_block = block_pair
        activations = trunk(window_block, mask_block, w_pre, biases, snake_params)
        return upsample(activations, mask_block[:, RIM:RIM + SEG], w_up, up_bias)

    outputs = lax.map(vocode, (windows.reshape(device_count, SLOT, SEG + 2 * RIM, FEAT),
                               window_masks.reshape(device_count, SLOT, SEG + 2 * RIM)))
    outputs = outputs.reshape(stream_len, SEG * UP, CH2)
    gathered = outputs[jnp.clip(position, 0, stream_len - 1)]
    return jnp.where((target >= 0)[:, None, None], gathered, jnp.zeros_like(gathered))
```

```python
import functools
import math

import jax
import jax.numpy as jnp
from jax import lax
from jax.experimental import pallas as pl
from jax.experimental.pallas import tpu as pltpu
from jax.sharding import PartitionSpec as P

UP = 4
KPRE = 7
RIM = 4
GROUP = 8
LANES = 128
MESH = pl.DeviceIdType.MESH
SIN2 = (9.8696029141, -32.4695807761, 42.7253786576, -30.0859046584, 12.9905554979, -3.2727110438)


def f32_dot(a, b):
    return jnp.dot(a, b, preferred_element_type=jnp.float32)


def hot(cond):
    return jnp.where(cond, 1.0, 0.0)


def exchange_kernel(
    groups, workers, slots,
    feat_ref, tcol_ref, trow_ref, ext_ref,
    win_ref, mask_ref,
    send, got, tail_tx, head_tx, prev_rx, next_rx, back, home,
    s1, r1, s2, r2, s3, r3,
):
    seg_len, cap, _ = feat_ref.shape
    rows = workers * 8
    width = 2 * RIM * LANES
    half = RIM * LANES
    gen = lax.axis_index("gen")
    voc = lax.axis_index("voc")
    count = groups * workers
    me = gen * workers + voc
    after = lax.rem(me + 1, count)
    before = lax.rem(me + count - 1, count)
    after_id = (lax.div(after, workers), lax.rem(after, workers))
    before_id = (lax.div(before, workers), lax.rem(before, workers))

    barrier = pltpu.get_barrier_semaphore()
    for d in range(1, workers):
        pl.semaphore_signal(
            barrier, inc=1, device_id=(gen, lax.rem(voc + d, workers)), device_id_type=MESH
        )
    for other in (after_id, before_id):
        pl.semaphore_signal(barrier, inc=1, device_id=other, device_id_type=MESH)

    tcol = tcol_ref[...]
    trow = trow_ref[...]
    i_c = lax.broadcasted_iota(jnp.int32, (cap, cap), 0)
    i_r = lax.broadcasted_iota(jnp.int32, (cap, cap), 1)
    used_c = tcol >= 0
    used_r = trow >= 0
    w_c = jnp.where(used_c, lax.div(jnp.maximum(tcol, 0), slots), -1)
    w_r = jnp.where(used_r, lax.div(jnp.maximum(trow, 0), slots), -1)
    same = (w_c == w_r) & used_r
    cnt_r = jnp.sum(hot(same & (i_c < i_r)), axis=0, keepdims=True).astype(jnp.int32)
    cnt_c = jnp.sum(hot(same & (i_r < i_c)), axis=1, keepdims=True).astype(jnp.int32)
    row_r = jnp.where(used_r[:1], w_r[:1] * 8 + cnt_r, -1)
    row_c = jnp.where(used_c[:, :1], w_c[:, :1] * 8 + cnt_c, -1)
    k_c = lax.broadcasted_iota(jnp.int32, (rows, cap), 0)
    k_r = lax.broadcasted_iota(jnp.int32, (cap, rows), 1)
    select = hot(k_c == row_r).astype(jnp.bfloat16)
    select_t = hot(k_r == row_c).astype(jnp.bfloat16)
    earlier = jnp.sum(hot(used_c & (i_c < i_r)), axis=0, keepdims=True).astype(jnp.int32)
    total = jnp.sum(hot(used_c), axis=0, keepdims=True).astype(jnp.int32)
    rank = jnp.where(used_r[:1], earlier, total + i_r[:1] - earlier)
    compact = hot(i_c == rank).astype(jnp.bfloat16)

    rims = list(range(RIM)) + list(range(seg_len - RIM, seg_len))
    for p, frame in enumerate(rims):
        part = f32_dot(select, feat_ref[frame])
        send[:, :, p * LANES : (p + 1) * LANES] = part.reshape(workers, 8, LANES).astype(
            jnp.bfloat16
        )
    slot_c = jnp.where(used_c, lax.rem(jnp.maximum(tcol, 0), slots) + 1, 0)
    slot_b = jnp.broadcast_to(slot_c[:, :1].astype(jnp.float32), (cap, LANES)).astype(jnp.bfloat16)
    send[:, :, width : width + LANES] = (
        f32_dot(select, slot_b).reshape(workers, 8, LANES).astype(jnp.bfloat16)
    )

    pl.semaphore_wait(barrier, workers + 1)

    def swap(src, dst, send_sem, recv_sem):
        copies = []
        for d in range(1, workers):
            peer = lax.rem(voc + d, workers)
            copy = pltpu.make_async_remote_copy(
                src_ref=src.at[peer],
                dst_ref=dst.at[voc],
                send_sem=send_sem.at[d],
                recv_sem=recv_sem.at[d],
                device_id=(gen, peer),
                device_id_type=MESH,
            )
            copy.start()
            copies.append(copy)
        dst[voc] = src[voc]
        return copies

    copies = swap(send, got, s1, r1)
    ext = [f32_dot(compact, ext_ref[k]) for k in range(3)]
    for t in range(RIM):
        mask_ref[t] = hot(ext[1] > t + seg_len - RIM + 0.5)
        mask_ref[RIM + seg_len + t] = hot(ext[2] > t + 0.5)
    for t in range(seg_len):
        valid = hot(ext[0] > t + 0.5)
        mask_ref[RIM + t] = valid
        win_ref[RIM + t] = f32_dot(compact, feat_ref[t]) * valid
    home_pick = f32_dot(compact, select_t).astype(jnp.bfloat16)
    for copy in copies:
        copy.wait()

    arrived = got[...].astype(jnp.float32).reshape(rows, width + LANES)
    slot_of = arrived[:, width:]
    lane = lax.broadcasted_iota(jnp.int32, (rows, LANES), 1).astype(jnp.float32)
    place = hot(slot_of == lane + 1.0).astype(jnp.bfloat16)
    canon = lax.dot_general(
        place,
        arrived[:, :width].astype(jnp.bfloat16),
        (((0,), (0,)), ((), ())),
        preferred_element_type=jnp.float32,
    )[:slots].astype(jnp.bfloat16)
    head_tx[...] = canon[:, :half]
    tail_tx[...] = canon[:, half:]
    shift = [
        pltpu.make_async_remote_copy(
            src_ref=src, dst_ref=dst, send_sem=s2.at[k], recv_sem=r2.at[k],
            device_id=other, device_id_type=MESH,
        )
        for k, (src, dst, other) in enumerate(
            ((tail_tx, prev_rx, after_id), (head_tx, next_rx, before_id))
        )
    ]
    for copy in shift:
        copy.start()
    held = slot_of > 0.5
    low = slot_of - 1.0 - jnp.where(me == 0, 1.0, 0.0)
    low = jnp.where(low < -0.5, low + float(slots), low)
    high = slot_of - 1.0 + jnp.where(me == count - 1, 1.0, 0.0)
    high = jnp.where(high > slots - 0.5, high - float(slots), high)
    place_prev = hot((low == lane) & held).astype(jnp.bfloat16)[:, :slots]
    place_next = hot((high == lane) & held).astype(jnp.bfloat16)[:, :slots]
    for copy in shift:
        copy.wait()
    back[:, :, :half] = (
        f32_dot(place_prev, prev_rx[...]).reshape(workers, 8, half).astype(jnp.bfloat16)
    )
    back[:, :, half:] = (
        f32_dot(place_next, next_rx[...]).reshape(workers, 8, half).astype(jnp.bfloat16)
    )
    copies = swap(back, home, s3, r3)
    for copy in copies:
        copy.wait()
    homed = home[...].astype(jnp.float32).reshape(rows, width).astype(jnp.bfloat16)
    both = f32_dot(home_pick, homed)
    for t in range(RIM):
        win_ref[t] = both[:, t * LANES : (t + 1) * LANES] * mask_ref[t]
        win_ref[RIM + seg_len + t] = (
            both[:, half + t * LANES : half + (t + 1) * LANES] * mask_ref[RIM + seg_len + t]
        )


def exchange(mesh, features, target, extents):
    cap, seg_len, width = features.shape
    slots = cap // 2
    workers, groups = mesh.shape["voc"], mesh.shape["gen"]
    span = seg_len + 2 * RIM
    feat = jnp.transpose(features, (1, 0, 2))
    tcol = jnp.broadcast_to(target[:, None], (cap, cap))
    trow = jnp.broadcast_to(target[None, :], (cap, cap))
    ext = jnp.broadcast_to(extents.T.astype(jnp.bfloat16)[:, :, None], (3, cap, LANES))
    vmem = pl.BlockSpec(memory_space=pltpu.VMEM)
    bf = jnp.bfloat16
    rim = RIM * width
    return pl.pallas_call(
        functools.partial(exchange_kernel, groups, workers, slots),
        out_shape=[jax.ShapeDtypeStruct((span, cap, width), jnp.float32)] * 2,
        in_specs=[vmem] * 4,
        out_specs=[vmem] * 2,
        scratch_shapes=[
            pltpu.VMEM((workers, 8, 2 * rim + LANES), bf),
            pltpu.VMEM((workers, 8, 2 * rim + LANES), bf),
            pltpu.VMEM((slots, rim), bf),
            pltpu.VMEM((slots, rim), bf),
            pltpu.VMEM((slots, rim), bf),
            pltpu.VMEM((slots, rim), bf),
            pltpu.VMEM((workers, 8, 2 * rim), bf),
            pltpu.VMEM((workers, 8, 2 * rim), bf),
            pltpu.SemaphoreType.DMA((workers,)),
            pltpu.SemaphoreType.DMA((workers,)),
            pltpu.SemaphoreType.DMA((2,)),
            pltpu.SemaphoreType.DMA((2,)),
            pltpu.SemaphoreType.DMA((workers,)),
            pltpu.SemaphoreType.DMA((workers,)),
        ],
        compiler_params=pltpu.CompilerParams(
            collective_id=0, has_side_effects=True, vmem_limit_bytes=24 * 2**20
        ),
        name="rim_exchange",
    )(feat, tcol, trow, ext)


def vocode_kernel(
    target_ref, win_ref, mask_ref, w_pre_ref, bias_ref, snake_ref, up_bias_ref, w_up_ref,
    out_ref,
    order, taps, stacked, act_even, act_odd, wave32, wave16, zeros, w_sem, z_sem, o_sem,
):
    span, cap, _ = win_ref.shape
    seg_len = span - 2 * RIM
    first = (KPRE - 1) // 2
    length = span - KPRE + 1
    ch = w_pre_ref.shape[1]
    ch2 = up_bias_ref.shape[1]
    samples = UP * seg_len

    loads = [
        pltpu.make_async_copy(
            w_up_ref.at[:, pl.ds(tap * ch2, ch2)], taps.at[tap], w_sem.at[tap]
        )
        for tap in range(2 * UP)
    ]
    for load in loads:
        load.start()

    def count_used(i, n):
        return n + jnp.where(target_ref[i] >= 0, 1, 0)

    used = lax.fori_loop(0, cap, count_used, 0)

    def place(i, state):
        a, b = state
        live = target_ref[i] >= 0
        order[jnp.where(live, a, b)] = i
        return a + jnp.where(live, 1, 0), b + jnp.where(live, 0, 1)

    lax.fori_loop(0, cap, place, (0, used))
    n_groups = lax.div(used + GROUP - 1, GROUP)

    zeros[...] = jnp.zeros_like(zeros)

    def zero_copy(i):
        return pltpu.make_async_copy(zeros, out_ref.at[order[i]], z_sem.at[i])

    @pl.loop(n_groups * GROUP, cap)
    def _(i):
        zero_copy(i).start()

    col = 256

    @pl.loop(0, n_groups)
    def _(g):
        at = pl.ds(pl.multiple_of(g * GROUP, GROUP), GROUP)
        for q in range(KPRE):
            stacked[:, q * LANES : (q + 1) * LANES] = (
                win_ref[q : q + length, at, :].reshape(length * GROUP, LANES).astype(jnp.bfloat16)
            )
        valid = mask_ref[first : first + length, at, :].reshape(length * GROUP, LANES)
        valid = jnp.concatenate([valid, valid], axis=1)
        for c in range(0, ch, col):
            cols = slice(c, c + col)
            hidden = valid * (
                f32_dot(stacked[...], w_pre_ref[:, cols]) + bias_ref[:, cols]
            )
            turns = hidden * (snake_ref[0:1, cols] * (1.0 / math.pi))
            part = turns - jnp.round(turns)
            z = part * part
            poly = jnp.full_like(z, SIN2[-1])
            for coeff in SIN2[-2::-1]:
                poly = poly * z + coeff
            act = hidden + (poly * z) * (1.0 / snake_ref[1:2, cols])
            act_even[g, :, cols] = act.astype(jnp.bfloat16)
            act_odd[g, :, cols] = act[GROUP : (seg_len + 1) * GROUP].astype(jnp.bfloat16)

    for load in loads:
        load.wait()

    def wave_copy(g, slot, k):
        return pltpu.make_async_copy(
            wave16.at[slot, k], out_ref.at[order[g * GROUP + k]], o_sem.at[slot, k]
        )

    @pl.loop(0, n_groups)
    def _(g):
        slot = lax.rem(g, 2)
        at = pl.ds(pl.multiple_of(g * GROUP, GROUP), GROUP)

        @pl.when(g >= 2)
        def _():
            for k in range(GROUP):
                wave_copy(g - 2, slot, k).wait()

        for c in range(0, ch2, col):
            cols = slice(c, c + col)
            for r in range(UP):
                if r < UP // 2:
                    side_at, side_tap = 0, r + 3 * UP // 2
                else:
                    side_at, side_tap = 2 * GROUP, r - UP // 2
                total = f32_dot(act_odd[g], taps[r + UP // 2, :, cols]) + f32_dot(
                    act_even[g, side_at : side_at + seg_len * GROUP, :], taps[side_tap, :, cols]
                )
                total = total + up_bias_ref[:, cols]
                for j in range(seg_len):
                    keep = mask_ref[RIM + j, at, :]
                    for h in range(col // LANES):
                        wave32[
                            pl.ds(
                                (c // LANES + h) * GROUP * samples + UP * j + r,
                                GROUP,
                                stride=samples,
                            ),
                            :,
                        ] = keep * total[j * GROUP : (j + 1) * GROUP, h * LANES : (h + 1) * LANES]
            for h in range(col // LANES):
                for k in range(GROUP):
                    start = ((c // LANES + h) * GROUP + k) * samples
                    wave16[slot, k, :, c + h * LANES : c + (h + 1) * LANES] = wave32[
                        start : start + samples, :
                    ].astype(jnp.bfloat16)
        for k in range(GROUP):
            wave_copy(g, slot, k).start()

    for lag in (2, 1):

        @pl.when(n_groups >= lag)
        def _():
            g = n_groups - lag
            for k in range(GROUP):
                wave_copy(g, lax.rem(g, 2), k).wait()

    @pl.loop(n_groups * GROUP, cap)
    def _(i):
        zero_copy(i).wait()


def vocode(target, window, mask, w_pre, biases, snake_params, w_up, up_bias):
    span, cap, width = window.shape
    seg_len = span - 2 * RIM
    ch, ch2 = w_pre.shape[1], up_bias.shape[0]
    length = span - KPRE + 1
    groups = cap // GROUP
    samples = UP * seg_len
    vmem = pl.BlockSpec(memory_space=pltpu.VMEM)
    hbm = pl.BlockSpec(memory_space=pl.ANY)
    rows = cap * seg_len
    return pl.pallas_call(
        vocode_kernel,
        out_shape=jax.ShapeDtypeStruct((cap, samples, ch2), jnp.bfloat16),
        in_specs=[pl.BlockSpec(memory_space=pltpu.SMEM)] + [vmem] * 6 + [hbm],
        out_specs=hbm,
        scratch_shapes=[
            pltpu.SMEM((cap,), jnp.int32),
            pltpu.VMEM((2 * UP, ch, ch2), jnp.bfloat16),
            pltpu.VMEM((length * GROUP, KPRE * width), jnp.bfloat16),
            pltpu.VMEM((groups, length * GROUP, ch), jnp.bfloat16),
            pltpu.VMEM((groups, seg_len * GROUP, ch), jnp.bfloat16),
            pltpu.VMEM((ch2 // LANES * GROUP * samples, LANES), jnp.float32),
            pltpu.VMEM((2, GROUP, samples, ch2), jnp.bfloat16),
            pltpu.VMEM((samples, ch2), jnp.bfloat16),
            pltpu.SemaphoreType.DMA((2 * UP,)),
            pltpu.SemaphoreType.DMA((cap,)),
            pltpu.SemaphoreType.DMA((2, GROUP)),
        ],
        compiler_params=pltpu.CompilerParams(vmem_limit_bytes=56 * 2**20),
        cost_estimate=pl.CostEstimate(
            flops=2 * rows * ch * (KPRE * width + 2 * UP * ch2),
            bytes_accessed=2 * (w_pre.size + w_up.size + rows * UP * ch2),
            transcendentals=0,
        ),
        name="vocode_used",
    )(target, window, mask, w_pre, biases[None], snake_params, up_bias[None], w_up)


def solution(mesh):
    def on_device(features, target, extents, w_pre, biases, snake_params, w_up, up_bias):
        window, mask = exchange(mesh, features, target, extents)
        return vocode(target, window, mask, w_pre, biases, snake_params, w_up, up_bias)

    placed = (
        P(("gen", "voc"), None, None),
        P(("gen", "voc")),
        P(("gen", "voc"), None),
        P(),
        P(),
        P(),
        P(),
        P(),
    )
    return jax.shard_map(
        on_device,
        mesh=mesh,
        in_specs=placed,
        out_specs=P(("gen", "voc"), None, None),
        check_vma=False,
    )
```

```python
import functools
import math

import jax
import jax.numpy as jnp
from jax import lax
from jax.experimental import pallas as pl
from jax.experimental.pallas import tpu as pltpu
from jax.sharding import PartitionSpec as P

UP = 4
KPRE = 7
RIM = 4
GROUP = 8
LANES = 128
MESH = pl.DeviceIdType.MESH
SIN2 = (9.8696029141, -32.4695807761, 42.7253786576, -30.0859046584, 12.9905554979, -3.2727110438)


def f32_dot(a, b):
    return jnp.dot(a, b, preferred_element_type=jnp.float32)


def hot(cond):
    return jnp.where(cond, 1.0, 0.0)


def exchange_kernel(
    groups, workers, slots,
    feat_ref, target_ref, ext_ref,
    win_ref, ext_out_ref,
    feat, window, send, got, tail_tx, head_tx, prev_rx, next_rx, back, home,
    s1, r1, s2, r2, s3, r3,
):
    cap, seg_len, _ = feat_ref.shape
    rows = workers * 8
    width = 2 * RIM * LANES
    half = RIM * LANES
    gen = lax.axis_index("gen")
    voc = lax.axis_index("voc")
    count = groups * workers
    me = gen * workers + voc
    after = lax.rem(me + 1, count)
    before = lax.rem(me + count - 1, count)
    after_id = (lax.div(after, workers), lax.rem(after, workers))
    before_id = (lax.div(before, workers), lax.rem(before, workers))

    barrier = pltpu.get_barrier_semaphore()
    for d in range(1, workers):
        pl.semaphore_signal(
            barrier, inc=1, device_id=(gen, lax.rem(voc + d, workers)), device_id_type=MESH
        )
    for other in (after_id, before_id):
        pl.semaphore_signal(barrier, inc=1, device_id=other, device_id_type=MESH)

    feat[...] = feat_ref[...].astype(jnp.float32).reshape(cap * seg_len, LANES)

    def frame_of(t):
        return feat[pl.ds(t, cap, stride=seg_len), :].astype(jnp.bfloat16)

    i_c = lax.broadcasted_iota(jnp.int32, (cap, cap), 0)
    i_r = lax.broadcasted_iota(jnp.int32, (cap, cap), 1)
    trow = jnp.broadcast_to(target_ref[...].reshape(1, cap), (cap, cap))
    tcol = jnp.sum(
        jnp.where(i_c == i_r, trow.astype(jnp.float32), 0.0), axis=1, keepdims=True
    ).astype(jnp.int32)
    tcol = jnp.broadcast_to(tcol, (cap, cap))
    used_c = tcol >= 0
    used_r = trow >= 0
    w_c = jnp.where(used_c, lax.div(jnp.maximum(tcol, 0), slots), -1)
    w_r = jnp.where(used_r, lax.div(jnp.maximum(trow, 0), slots), -1)
    same = (w_c == w_r) & used_r
    cnt_r = jnp.sum(hot(same & (i_c < i_r)), axis=0, keepdims=True).astype(jnp.int32)
    cnt_c = jnp.sum(hot(same & (i_r < i_c)), axis=1, keepdims=True).astype(jnp.int32)
    row_r = jnp.where(used_r[:1], w_r[:1] * 8 + cnt_r, -1)
    row_c = jnp.where(used_c[:, :1], w_c[:, :1] * 8 + cnt_c, -1)
    k_c = lax.broadcasted_iota(jnp.int32, (rows, cap), 0)
    k_r = lax.broadcasted_iota(jnp.int32, (cap, rows), 1)
    select = hot(k_c == row_r).astype(jnp.bfloat16)
    select_t = hot(k_r == row_c).astype(jnp.bfloat16)
    earlier = jnp.sum(hot(used_c & (i_c < i_r)), axis=0, keepdims=True).astype(jnp.int32)
    total = jnp.sum(hot(used_c), axis=0, keepdims=True).astype(jnp.int32)
    rank = jnp.where(used_r[:1], earlier, total + i_r[:1] - earlier)
    compact = hot(i_c == rank).astype(jnp.bfloat16)

    rims = list(range(RIM)) + list(range(seg_len - RIM, seg_len))
    for p, frame in enumerate(rims):
        part = f32_dot(select, frame_of(frame))
        send[:, :, p * LANES : (p + 1) * LANES] = part.reshape(workers, 8, LANES).astype(
            jnp.bfloat16
        )
    slot_c = jnp.where(used_c, lax.rem(jnp.maximum(tcol, 0), slots) + 1, 0)
    slot_b = jnp.broadcast_to(slot_c[:, :1].astype(jnp.float32), (cap, LANES)).astype(jnp.bfloat16)
    send[:, :, width : width + LANES] = (
        f32_dot(select, slot_b).reshape(workers, 8, LANES).astype(jnp.bfloat16)
    )

    pl.semaphore_wait(barrier, workers + 1)

    def swap(src, dst, send_sem, recv_sem):
        copies = []
        for d in range(1, workers):
            peer = lax.rem(voc + d, workers)
            copy = pltpu.make_async_remote_copy(
                src_ref=src.at[peer],
                dst_ref=dst.at[voc],
                send_sem=send_sem.at[d],
                recv_sem=recv_sem.at[d],
                device_id=(gen, peer),
                device_id_type=MESH,
            )
            copy.start()
            copies.append(copy)
        dst[voc] = src[voc]
        return copies

    copies = swap(send, got, s1, r1)
    picked = hot(i_c == rank)
    ext = []
    for k in range(3):
        row = ext_ref[k : k + 1, :].astype(jnp.float32)
        ext.append(
            jnp.broadcast_to(jnp.sum(picked * row, axis=1, keepdims=True), (cap, LANES))
        )
        ext_out_ref[k] = ext[k]
    for t in range(seg_len):
        window[RIM + t] = f32_dot(compact, frame_of(t)) * hot(ext[0] > t + 0.5)
    home_pick = f32_dot(compact, select_t).astype(jnp.bfloat16)
    for copy in copies:
        copy.wait()

    arrived = got[...].astype(jnp.float32).reshape(rows, width + LANES)
    slot_of = arrived[:, width:]
    lane = lax.broadcasted_iota(jnp.int32, (rows, LANES), 1).astype(jnp.float32)
    place = hot(slot_of == lane + 1.0).astype(jnp.bfloat16)
    canon = lax.dot_general(
        place,
        arrived[:, :width].astype(jnp.bfloat16),
        (((0,), (0,)), ((), ())),
        preferred_element_type=jnp.float32,
    )[:slots].astype(jnp.bfloat16)
    head_tx[...] = canon[:, :half]
    tail_tx[...] = canon[:, half:]
    shift = [
        pltpu.make_async_remote_copy(
            src_ref=src, dst_ref=dst, send_sem=s2.at[k], recv_sem=r2.at[k],
            device_id=other, device_id_type=MESH,
        )
        for k, (src, dst, other) in enumerate(
            ((tail_tx, prev_rx, after_id), (head_tx, next_rx, before_id))
        )
    ]
    for copy in shift:
        copy.start()
    held = slot_of > 0.5
    low = slot_of - 1.0 - jnp.where(me == 0, 1.0, 0.0)
    low = jnp.where(low < -0.5, low + float(slots), low)
    high = slot_of - 1.0 + jnp.where(me == count - 1, 1.0, 0.0)
    high = jnp.where(high > slots - 0.5, high - float(slots), high)
    place_prev = hot((low == lane) & held).astype(jnp.bfloat16)[:, :slots]
    place_next = hot((high == lane) & held).astype(jnp.bfloat16)[:, :slots]
    for copy in shift:
        copy.wait()
    back[:, :, :half] = (
        f32_dot(place_prev, prev_rx[...]).reshape(workers, 8, half).astype(jnp.bfloat16)
    )
    back[:, :, half:] = (
        f32_dot(place_next, next_rx[...]).reshape(workers, 8, half).astype(jnp.bfloat16)
    )
    copies = swap(back, home, s3, r3)
    for copy in copies:
        copy.wait()
    homed = home[...].astype(jnp.float32).reshape(rows, width).astype(jnp.bfloat16)
    both = f32_dot(home_pick, homed)
    for t in range(RIM):
        window[t] = both[:, t * LANES : (t + 1) * LANES] * hot(ext[1] > t + seg_len - RIM + 0.5)
        window[RIM + seg_len + t] = both[:, half + t * LANES : half + (t + 1) * LANES] * hot(
            ext[2] > t + 0.5
        )
    span = seg_len + 2 * RIM
    for g in range(cap // GROUP):
        win_ref[g] = (
            window[:, g * GROUP : (g + 1) * GROUP, :]
            .reshape(span * GROUP, LANES)
            .astype(jnp.bfloat16)
        )


def exchange(mesh, features, target, extents):
    cap, seg_len, width = features.shape
    slots = cap // 2
    workers, groups = mesh.shape["voc"], mesh.shape["gen"]
    span = seg_len + 2 * RIM
    vmem = pl.BlockSpec(memory_space=pltpu.VMEM)
    bf = jnp.bfloat16
    rim = RIM * width
    return pl.pallas_call(
        functools.partial(exchange_kernel, groups, workers, slots),
        out_shape=[
            jax.ShapeDtypeStruct((cap // GROUP, span * GROUP, width), bf),
            jax.ShapeDtypeStruct((3, cap, LANES), jnp.float32),
        ],
        in_specs=[vmem] * 3,
        out_specs=[vmem] * 2,
        scratch_shapes=[
            pltpu.VMEM((cap * seg_len, width), jnp.float32),
            pltpu.VMEM((span, cap, width), jnp.float32),
            pltpu.VMEM((workers, 8, 2 * rim + LANES), bf),
            pltpu.VMEM((workers, 8, 2 * rim + LANES), bf),
            pltpu.VMEM((slots, rim), bf),
            pltpu.VMEM((slots, rim), bf),
            pltpu.VMEM((slots, rim), bf),
            pltpu.VMEM((slots, rim), bf),
            pltpu.VMEM((workers, 8, 2 * rim), bf),
            pltpu.VMEM((workers, 8, 2 * rim), bf),
            pltpu.SemaphoreType.DMA((workers,)),
            pltpu.SemaphoreType.DMA((workers,)),
            pltpu.SemaphoreType.DMA((2,)),
            pltpu.SemaphoreType.DMA((2,)),
            pltpu.SemaphoreType.DMA((workers,)),
            pltpu.SemaphoreType.DMA((workers,)),
        ],
        compiler_params=pltpu.CompilerParams(
            collective_id=0, has_side_effects=True, vmem_limit_bytes=24 * 2**20
        ),
        name="rim_exchange",
    )(features, target, extents.T)


def vocode_kernel(
    target_ref, win_ref, ext_ref, w_pre_ref, bias_ref, snake_ref, up_bias_ref, w_up_ref,
    out_ref,
    order, taps, stacked, act_even, act_odd, wave32, wave16, zeros, w_sem, z_sem, o_sem,
):
    cap = target_ref.shape[0]
    span = win_ref.shape[1] // GROUP
    seg_len = span - 2 * RIM
    first = (KPRE - 1) // 2
    length = span - KPRE + 1
    ch = w_pre_ref.shape[1]
    ch2 = up_bias_ref.shape[0]
    samples = UP * seg_len
    col = 256

    def centre_tap(r):
        return r + UP // 2

    def side_tap(r):
        return r + 3 * UP // 2 if r < UP // 2 else r - UP // 2

    def load(tap):
        return pltpu.make_async_copy(
            w_up_ref.at[:, pl.ds(tap * ch2, ch2)], taps.at[tap], w_sem.at[tap]
        )

    for r in range(UP):
        load(centre_tap(r)).start()
        load(side_tap(r)).start()

    def place(i, state):
        a, b = state
        live = jnp.where(target_ref[i] >= 0, 1, 0)
        order[jnp.where(live == 1, a, b)] = i
        return a + live, b - 1 + live

    used, _ = lax.fori_loop(0, cap, place, (0, cap - 1), unroll=True)
    n_groups = lax.div(used + GROUP - 1, GROUP)

    zeros[...] = jnp.zeros_like(zeros)

    def zero_copy(i):
        return pltpu.make_async_copy(zeros, out_ref.at[order[i]], z_sem.at[i])

    @pl.loop(n_groups * GROUP, cap)
    def _(i):
        zero_copy(i).start()

    def frame_mask(g, t):
        at = pl.ds(pl.multiple_of(g * GROUP, GROUP), GROUP)
        if t < RIM:
            return hot(ext_ref[1, at, :] > t + seg_len - RIM + 0.5)
        if t < RIM + seg_len:
            return hot(ext_ref[0, at, :] > t - RIM + 0.5)
        return hot(ext_ref[2, at, :] > t - RIM - seg_len + 0.5)

    @pl.loop(0, n_groups)
    def _(g):
        frames = win_ref[g].astype(jnp.float32)
        for q in range(KPRE):
            stacked[:, q * LANES : (q + 1) * LANES] = frames[
                q * GROUP : (q + length) * GROUP
            ].astype(jnp.bfloat16)
        valid = jnp.concatenate([frame_mask(g, first + t) for t in range(length)], axis=0)
        valid = jnp.concatenate([valid, valid], axis=1)
        for c in range(0, ch, col):
            cols = slice(c, c + col)
            bias = bias_ref[cols].reshape(1, col)
            hidden = valid * (f32_dot(stacked[...], w_pre_ref[:, cols]) + bias)
            turns = hidden * (snake_ref[0:1, cols] * (1.0 / math.pi))
            part = turns - jnp.round(turns)
            z = part * part
            poly = jnp.full_like(z, SIN2[-1])
            for coeff in SIN2[-2::-1]:
                poly = poly * z + coeff
            act = hidden + (poly * z) * (1.0 / snake_ref[1:2, cols])
            act_even[g, :, cols] = act.astype(jnp.bfloat16)
            act_odd[g, :, cols] = act[GROUP : (seg_len + 1) * GROUP].astype(jnp.bfloat16)

    def wave_copy(g, slot, k):
        return pltpu.make_async_copy(
            wave16.at[slot, k], out_ref.at[order[g * GROUP + k]], o_sem.at[slot, k]
        )

    def upsample(g, slot, many, fresh):
        for r in range(UP):
            if fresh is not None:

                @pl.when(fresh)
                def _():
                    load(centre_tap(r)).wait()
                    load(side_tap(r)).wait()

            side_at = 0 if r < UP // 2 else 2 * GROUP
            rows = seg_len * GROUP
            lhs = jnp.concatenate(
                [
                    jnp.concatenate(
                        [act_odd[g + m], act_even[g + m, side_at : side_at + rows, :]], axis=1
                    )
                    for m in range(many)
                ],
                axis=0,
            )
            for c in range(0, ch2, col):
                cols = slice(c, c + col)
                rhs = jnp.concatenate(
                    [taps[centre_tap(r), :, cols], taps[side_tap(r), :, cols]], axis=0
                )
                total = f32_dot(lhs, rhs) + up_bias_ref[cols].reshape(1, col)
                for m in range(many):
                    for j in range(seg_len):
                        keep = frame_mask(g + m, RIM + j)
                        at = (m * seg_len + j) * GROUP
                        for h in range(col // LANES):
                            block = (m * (ch2 // LANES) + c // LANES + h) * GROUP
                            wave32[pl.ds(block * samples + UP * j + r, GROUP, stride=samples), :] = (
                                keep * total[at : at + GROUP, h * LANES : (h + 1) * LANES]
                            )
                if r == UP - 1:
                    for m in range(many):
                        for h in range(c // LANES, (c + col) // LANES):
                            for k in range(GROUP):
                                start = ((m * (ch2 // LANES) + h) * GROUP + k) * samples
                                wave16[
                                    slot, m * GROUP + k, :, h * LANES : (h + 1) * LANES
                                ] = wave32[start : start + samples, :].astype(jnp.bfloat16)
        for k in range(many * GROUP):
            wave_copy(g, slot, k).start()

    pairs = lax.div(n_groups, 2)
    odd = lax.rem(n_groups, 2)

    @pl.loop(0, pairs)
    def _(p):
        slot = lax.rem(p, 2)

        @pl.when(p >= 2)
        def _():
            for k in range(2 * GROUP):
                wave_copy(2 * p - 4, slot, k).wait()

        upsample(2 * p, slot, 2, p == 0)

    @pl.when(pairs == 0)
    def _():
        for r in range(UP):
            load(centre_tap(r)).wait()
            load(side_tap(r)).wait()

    @pl.when(pairs >= 2)
    def _():
        for k in range(2 * GROUP):
            wave_copy(2 * pairs - 4, lax.rem(pairs, 2), k).wait()

    @pl.when(odd == 1)
    def _():
        upsample(n_groups - 1, lax.rem(pairs, 2), 1, None)

    @pl.when(pairs >= 1)
    def _():
        for k in range(2 * GROUP):
            wave_copy(2 * pairs - 2, lax.rem(pairs + 1, 2), k).wait()

    @pl.when(odd == 1)
    def _():
        for k in range(GROUP):
            wave_copy(n_groups - 1, lax.rem(pairs, 2), k).wait()

    @pl.loop(n_groups * GROUP, cap)
    def _(i):
        zero_copy(i).wait()


def vocode(target, window, ext, w_pre, biases, snake_params, w_up, up_bias):
    cap, width = target.shape[0], window.shape[2]
    span = window.shape[1] // GROUP
    seg_len = span - 2 * RIM
    ch, ch2 = w_pre.shape[1], up_bias.shape[0]
    length = span - KPRE + 1
    groups = cap // GROUP
    samples = UP * seg_len
    vmem = pl.BlockSpec(memory_space=pltpu.VMEM)
    hbm = pl.BlockSpec(memory_space=pl.ANY)
    rows = cap * seg_len
    return pl.pallas_call(
        vocode_kernel,
        out_shape=jax.ShapeDtypeStruct((cap, samples, ch2), jnp.bfloat16),
        in_specs=[pl.BlockSpec(memory_space=pltpu.SMEM)] + [vmem] * 6 + [hbm],
        out_specs=hbm,
        scratch_shapes=[
            pltpu.SMEM((cap,), jnp.int32),
            pltpu.VMEM((2 * UP, ch, ch2), jnp.bfloat16),
            pltpu.VMEM((length * GROUP, KPRE * width), jnp.bfloat16),
            pltpu.VMEM((groups, length * GROUP, ch), jnp.bfloat16),
            pltpu.VMEM((groups, seg_len * GROUP, ch), jnp.bfloat16),
            pltpu.VMEM((2 * ch2 // LANES * GROUP * samples, LANES), jnp.float32),
            pltpu.VMEM((2, 2 * GROUP, samples, ch2), jnp.bfloat16),
            pltpu.VMEM((samples, ch2), jnp.bfloat16),
            pltpu.SemaphoreType.DMA((2 * UP,)),
            pltpu.SemaphoreType.DMA((cap,)),
            pltpu.SemaphoreType.DMA((2, 2 * GROUP)),
        ],
        compiler_params=pltpu.CompilerParams(vmem_limit_bytes=48 * 2**20),
        cost_estimate=pl.CostEstimate(
            flops=2 * rows * ch * (KPRE * width + 2 * UP * ch2),
            bytes_accessed=2 * (w_pre.size + w_up.size + rows * UP * ch2),
            transcendentals=0,
        ),
        name="vocode_used",
    )(target, window, ext, w_pre, biases, snake_params, up_bias, w_up)


def solution(mesh):
    def on_device(features, target, extents, w_pre, biases, snake_params, w_up, up_bias):
        window, ext = exchange(mesh, features, target, extents)
        return vocode(target, window, ext, w_pre, biases, snake_params, w_up, up_bias)

    placed = (
        P(("gen", "voc"), None, None),
        P(("gen", "voc")),
        P(("gen", "voc"), None),
        P(),
        P(),
        P(),
        P(),
        P(),
    )
    return jax.shard_map(
        on_device,
        mesh=mesh,
        in_specs=placed,
        out_specs=P(("gen", "voc"), None, None),
        check_vma=False,
    )
```

```python
import functools
import math

import jax
import jax.numpy as jnp
from jax import lax
from jax.experimental import pallas as pl
from jax.experimental.pallas import tpu as pltpu
from jax.sharding import PartitionSpec as P

UP = 4
KPRE = 7
RIM = 4
GROUP = 8
LANES = 128
MESH = pl.DeviceIdType.MESH
SIN2 = (9.8696029141, -32.4695807761, 42.7253786576, -30.0859046584, 12.9905554979, -3.2727110438)


def f32_dot(a, b):
    return jnp.dot(a, b, preferred_element_type=jnp.float32)


def hot(cond):
    return jnp.where(cond, 1.0, 0.0)


def exchange_kernel(
    groups, workers, slots,
    feat_ref, target_ref, ext_ref,
    win_ref, ext_out_ref,
    feat, window, send, got, tail_tx, head_tx, prev_rx, next_rx, back, home,
    s1, r1, s2, r2, s3, r3,
):
    cap, seg_len, _ = feat_ref.shape
    rows = workers * 8
    width = 2 * RIM * LANES
    half = RIM * LANES
    gen = lax.axis_index("gen")
    voc = lax.axis_index("voc")
    count = groups * workers
    me = gen * workers + voc
    after = lax.rem(me + 1, count)
    before = lax.rem(me + count - 1, count)
    after_id = (lax.div(after, workers), lax.rem(after, workers))
    before_id = (lax.div(before, workers), lax.rem(before, workers))

    barrier = pltpu.get_barrier_semaphore()
    for d in range(1, workers):
        pl.semaphore_signal(
            barrier, inc=1, device_id=(gen, lax.rem(voc + d, workers)), device_id_type=MESH
        )
    for other in (after_id, before_id):
        pl.semaphore_signal(barrier, inc=1, device_id=other, device_id_type=MESH)

    feat[...] = feat_ref[...].astype(jnp.float32).reshape(cap * seg_len, LANES)

    def frame_of(t):
        return feat[pl.ds(t, cap, stride=seg_len), :].astype(jnp.bfloat16)

    i_c = lax.broadcasted_iota(jnp.int32, (cap, cap), 0)
    i_r = lax.broadcasted_iota(jnp.int32, (cap, cap), 1)
    trow = jnp.broadcast_to(target_ref[...].reshape(1, cap), (cap, cap))
    tcol = jnp.sum(
        jnp.where(i_c == i_r, trow.astype(jnp.float32), 0.0), axis=1, keepdims=True
    ).astype(jnp.int32)
    tcol = jnp.broadcast_to(tcol, (cap, cap))
    used_c = tcol >= 0
    used_r = trow >= 0
    w_c = jnp.where(used_c, lax.div(jnp.maximum(tcol, 0), slots), -1)
    w_r = jnp.where(used_r, lax.div(jnp.maximum(trow, 0), slots), -1)
    same = (w_c == w_r) & used_r
    cnt_r = jnp.sum(hot(same & (i_c < i_r)), axis=0, keepdims=True).astype(jnp.int32)
    cnt_c = jnp.sum(hot(same & (i_r < i_c)), axis=1, keepdims=True).astype(jnp.int32)
    row_r = jnp.where(used_r[:1], w_r[:1] * 8 + cnt_r, -1)
    row_c = jnp.where(used_c[:, :1], w_c[:, :1] * 8 + cnt_c, -1)
    k_c = lax.broadcasted_iota(jnp.int32, (rows, cap), 0)
    k_r = lax.broadcasted_iota(jnp.int32, (cap, rows), 1)
    select = hot(k_c == row_r).astype(jnp.bfloat16)
    select_t = hot(k_r == row_c).astype(jnp.bfloat16)
    earlier = jnp.sum(hot(used_c & (i_c < i_r)), axis=0, keepdims=True).astype(jnp.int32)
    total = jnp.sum(hot(used_c), axis=0, keepdims=True).astype(jnp.int32)
    rank = jnp.where(used_r[:1], earlier, total + i_r[:1] - earlier)
    compact = hot(i_c == rank).astype(jnp.bfloat16)

    slot_c = jnp.where(used_c, lax.rem(jnp.maximum(tcol, 0), slots) + 1, 0)
    slot_b = jnp.broadcast_to(slot_c[:, :1].astype(jnp.float32), (cap, LANES)).astype(jnp.bfloat16)
    rims = list(range(RIM)) + list(range(seg_len - RIM, seg_len))
    parts = jnp.concatenate([frame_of(frame) for frame in rims] + [slot_b], axis=1)
    send[...] = (
        f32_dot(select, parts).reshape(workers, 8, width + LANES).astype(jnp.bfloat16)
    )

    pl.semaphore_wait(barrier, workers + 1)

    def swap(src, dst, send_sem, recv_sem):
        copies = []
        for d in range(1, workers):
            peer = lax.rem(voc + d, workers)
            copy = pltpu.make_async_remote_copy(
                src_ref=src.at[peer],
                dst_ref=dst.at[voc],
                send_sem=send_sem.at[d],
                recv_sem=recv_sem.at[d],
                device_id=(gen, peer),
                device_id_type=MESH,
            )
            copy.start()
            copies.append(copy)
        dst[voc] = src[voc]
        return copies

    copies = swap(send, got, s1, r1)
    picked = hot(i_c == rank)
    ext = []
    for k in range(3):
        row = ext_ref[k : k + 1, :].astype(jnp.float32)
        ext.append(
            jnp.broadcast_to(jnp.sum(picked * row, axis=1, keepdims=True), (cap, LANES))
        )
        ext_out_ref[k] = ext[k]
    for t in range(0, seg_len, 8):
        own = f32_dot(compact, jnp.concatenate([frame_of(t + i) for i in range(8)], axis=1))
        for i in range(8):
            window[RIM + t + i] = own[:, i * LANES : (i + 1) * LANES] * hot(ext[0] > t + i + 0.5)
    home_pick = f32_dot(compact, select_t).astype(jnp.bfloat16)
    for copy in copies:
        copy.wait()

    arrived = got[...].astype(jnp.float32).reshape(rows, width + LANES)
    slot_of = arrived[:, width:]
    lane = lax.broadcasted_iota(jnp.int32, (rows, LANES), 1).astype(jnp.float32)
    place = hot(slot_of == lane + 1.0).astype(jnp.bfloat16)
    canon = lax.dot_general(
        place,
        arrived[:, :width].astype(jnp.bfloat16),
        (((0,), (0,)), ((), ())),
        preferred_element_type=jnp.float32,
    )[:slots].astype(jnp.bfloat16)
    head_tx[...] = canon[:, :half]
    tail_tx[...] = canon[:, half:]
    shift = [
        pltpu.make_async_remote_copy(
            src_ref=src, dst_ref=dst, send_sem=s2.at[k], recv_sem=r2.at[k],
            device_id=other, device_id_type=MESH,
        )
        for k, (src, dst, other) in enumerate(
            ((tail_tx, prev_rx, after_id), (head_tx, next_rx, before_id))
        )
    ]
    for copy in shift:
        copy.start()
    held = slot_of > 0.5
    low = slot_of - 1.0 - jnp.where(me == 0, 1.0, 0.0)
    low = jnp.where(low < -0.5, low + float(slots), low)
    high = slot_of - 1.0 + jnp.where(me == count - 1, 1.0, 0.0)
    high = jnp.where(high > slots - 0.5, high - float(slots), high)
    place_prev = hot((low == lane) & held).astype(jnp.bfloat16)[:, :slots]
    place_next = hot((high == lane) & held).astype(jnp.bfloat16)[:, :slots]
    for copy in shift:
        copy.wait()
    back[:, :, :half] = (
        f32_dot(place_prev, prev_rx[...]).reshape(workers, 8, half).astype(jnp.bfloat16)
    )
    back[:, :, half:] = (
        f32_dot(place_next, next_rx[...]).reshape(workers, 8, half).astype(jnp.bfloat16)
    )
    copies = swap(back, home, s3, r3)
    for copy in copies:
        copy.wait()
    homed = home[...].astype(jnp.float32).reshape(rows, width).astype(jnp.bfloat16)
    both = f32_dot(home_pick, homed)
    for t in range(RIM):
        window[t] = both[:, t * LANES : (t + 1) * LANES] * hot(ext[1] > t + seg_len - RIM + 0.5)
        window[RIM + seg_len + t] = both[:, half + t * LANES : half + (t + 1) * LANES] * hot(
            ext[2] > t + 0.5
        )
    span = seg_len + 2 * RIM
    for g in range(cap // GROUP):
        win_ref[g] = (
            window[:, g * GROUP : (g + 1) * GROUP, :]
            .reshape(span * GROUP, LANES)
            .astype(jnp.bfloat16)
        )


def exchange(mesh, features, target, extents):
    cap, seg_len, width = features.shape
    slots = cap // 2
    workers, groups = mesh.shape["voc"], mesh.shape["gen"]
    span = seg_len + 2 * RIM
    vmem = pl.BlockSpec(memory_space=pltpu.VMEM)
    bf = jnp.bfloat16
    rim = RIM * width
    return pl.pallas_call(
        functools.partial(exchange_kernel, groups, workers, slots),
        out_shape=[
            jax.ShapeDtypeStruct((cap // GROUP, span * GROUP, width), bf),
            jax.ShapeDtypeStruct((3, cap, LANES), jnp.float32),
        ],
        in_specs=[vmem] * 3,
        out_specs=[vmem] * 2,
        scratch_shapes=[
            pltpu.VMEM((cap * seg_len, width), jnp.float32),
            pltpu.VMEM((span, cap, width), jnp.float32),
            pltpu.VMEM((workers, 8, 2 * rim + LANES), bf),
            pltpu.VMEM((workers, 8, 2 * rim + LANES), bf),
            pltpu.VMEM((slots, rim), bf),
            pltpu.VMEM((slots, rim), bf),
            pltpu.VMEM((slots, rim), bf),
            pltpu.VMEM((slots, rim), bf),
            pltpu.VMEM((workers, 8, 2 * rim), bf),
            pltpu.VMEM((workers, 8, 2 * rim), bf),
            pltpu.SemaphoreType.DMA((workers,)),
            pltpu.SemaphoreType.DMA((workers,)),
            pltpu.SemaphoreType.DMA((2,)),
            pltpu.SemaphoreType.DMA((2,)),
            pltpu.SemaphoreType.DMA((workers,)),
            pltpu.SemaphoreType.DMA((workers,)),
        ],
        compiler_params=pltpu.CompilerParams(
            collective_id=0, has_side_effects=True, vmem_limit_bytes=56 * 2**20
        ),
        name="rim_exchange",
    )(features, target, extents.T)


def vocode_kernel(
    target_ref, win_ref, ext_ref, w_pre_ref, bias_ref, snake_ref, up_bias_ref, w_up_ref,
    out_ref,
    order, taps, stacked, act_even, act_odd, wave32, wave16, zeros, w_sem, z_sem, o_sem,
):
    cap = target_ref.shape[0]
    span = win_ref.shape[1] // GROUP
    seg_len = span - 2 * RIM
    first = (KPRE - 1) // 2
    length = span - KPRE + 1
    ch = w_pre_ref.shape[1]
    ch2 = up_bias_ref.shape[0]
    samples = UP * seg_len
    col = 256

    def centre_tap(r):
        return r + UP // 2

    def side_tap(r):
        return r + 3 * UP // 2 if r < UP // 2 else r - UP // 2

    def load(tap):
        return pltpu.make_async_copy(
            w_up_ref.at[:, pl.ds(tap * ch2, ch2)], taps.at[tap], w_sem.at[tap]
        )

    for r in range(UP):
        load(centre_tap(r)).start()
        load(side_tap(r)).start()

    def place(i, state):
        a, b = state
        live = jnp.where(target_ref[i] >= 0, 1, 0)
        order[jnp.where(live == 1, a, b)] = i
        return a + live, b - 1 + live

    used, _ = lax.fori_loop(0, cap, place, (0, cap - 1), unroll=True)
    n_groups = lax.div(used + GROUP - 1, GROUP)

    zeros[...] = jnp.zeros_like(zeros)

    def zero_copy(i):
        return pltpu.make_async_copy(zeros, out_ref.at[order[i]], z_sem.at[i])

    @pl.loop(n_groups * GROUP, cap)
    def _(i):
        zero_copy(i).start()

    def frame_mask(g, t):
        at = pl.ds(pl.multiple_of(g * GROUP, GROUP), GROUP)
        if t < RIM:
            return hot(ext_ref[1, at, :] > t + seg_len - RIM + 0.5)
        if t < RIM + seg_len:
            return hot(ext_ref[0, at, :] > t - RIM + 0.5)
        return hot(ext_ref[2, at, :] > t - RIM - seg_len + 0.5)

    @pl.loop(0, n_groups)
    def _(g):
        frames = win_ref[g].astype(jnp.float32)
        for q in range(KPRE):
            stacked[:, q * LANES : (q + 1) * LANES] = frames[
                q * GROUP : (q + length) * GROUP
            ].astype(jnp.bfloat16)
        valid = jnp.concatenate([frame_mask(g, first + t) for t in range(length)], axis=0)
        valid = jnp.concatenate([valid, valid], axis=1)

        @pl.loop(0, ch // col)
        def _(c):
            cols = pl.ds(pl.multiple_of(c * col, col), col)
            bias = bias_ref[cols].reshape(1, col)
            hidden = valid * (f32_dot(stacked[...], w_pre_ref[:, cols]) + bias)
            turns = hidden * (snake_ref[0:1, cols] * (1.0 / math.pi))
            part = turns - jnp.round(turns)
            z = part * part
            poly = jnp.full_like(z, SIN2[-1])
            for coeff in SIN2[-2::-1]:
                poly = poly * z + coeff
            act = hidden + (poly * z) * (1.0 / snake_ref[1:2, cols])
            act_even[g, :, cols] = act.astype(jnp.bfloat16)
            act_odd[g, :, cols] = act[GROUP : (seg_len + 1) * GROUP].astype(jnp.bfloat16)

    for r in range(UP):
        load(centre_tap(r)).wait()
        load(side_tap(r)).wait()

    def wave_copy(g, slot, k):
        return pltpu.make_async_copy(
            wave16.at[slot, k], out_ref.at[order[g * GROUP + k]], o_sem.at[slot, k]
        )

    rows = seg_len * GROUP

    @pl.loop(0, n_groups)
    def _(g):
        slot = lax.rem(g, 2)

        @pl.when(g >= 2)
        def _():
            for k in range(GROUP):
                wave_copy(g - 2, slot, k).wait()

        @pl.loop(0, ch2 // col)
        def _(c):
            cols = pl.ds(pl.multiple_of(c * col, col), col)
            bias = up_bias_ref[cols].reshape(1, col)
            for r in range(UP):
                side_at = 0 if r < UP // 2 else 2 * GROUP
                lhs = jnp.concatenate(
                    [act_odd[g], act_even[g, side_at : side_at + rows, :]], axis=1
                )
                rhs = jnp.concatenate(
                    [taps[centre_tap(r), :, cols], taps[side_tap(r), :, cols]], axis=0
                )
                total = f32_dot(lhs, rhs) + bias
                for j in range(seg_len):
                    keep = frame_mask(g, RIM + j)
                    for h in range(col // LANES):
                        wave32[
                            pl.ds(h * GROUP * samples + UP * j + r, GROUP, stride=samples), :
                        ] = keep * total[j * GROUP : (j + 1) * GROUP, h * LANES : (h + 1) * LANES]
            for h in range(col // LANES):
                lanes = pl.ds(pl.multiple_of(c * col + h * LANES, LANES), LANES)
                for k in range(GROUP):
                    start = (h * GROUP + k) * samples
                    wave16[slot, k, :, lanes] = wave32[start : start + samples, :].astype(
                        jnp.bfloat16
                    )

        for k in range(GROUP):
            wave_copy(g, slot, k).start()

    for lag in (2, 1):

        @pl.when(n_groups >= lag)
        def _():
            g = n_groups - lag
            for k in range(GROUP):
                wave_copy(g, lax.rem(g, 2), k).wait()

    @pl.loop(n_groups * GROUP, cap)
    def _(i):
        zero_copy(i).wait()


def vocode(target, window, ext, w_pre, biases, snake_params, w_up, up_bias):
    cap, width = target.shape[0], window.shape[2]
    span = window.shape[1] // GROUP
    seg_len = span - 2 * RIM
    ch, ch2 = w_pre.shape[1], up_bias.shape[0]
    length = span - KPRE + 1
    groups = cap // GROUP
    samples = UP * seg_len
    vmem = pl.BlockSpec(memory_space=pltpu.VMEM)
    hbm = pl.BlockSpec(memory_space=pl.ANY)
    rows = cap * seg_len
    return pl.pallas_call(
        vocode_kernel,
        out_shape=jax.ShapeDtypeStruct((cap, samples, ch2), jnp.bfloat16),
        in_specs=[pl.BlockSpec(memory_space=pltpu.SMEM)] + [vmem] * 6 + [hbm],
        out_specs=hbm,
        scratch_shapes=[
            pltpu.SMEM((cap,), jnp.int32),
            pltpu.VMEM((2 * UP, ch, ch2), jnp.bfloat16),
            pltpu.VMEM((length * GROUP, KPRE * width), jnp.bfloat16),
            pltpu.VMEM((groups, length * GROUP, ch), jnp.bfloat16),
            pltpu.VMEM((groups, seg_len * GROUP, ch), jnp.bfloat16),
            pltpu.VMEM((256 // LANES * GROUP * samples, LANES), jnp.float32),
            pltpu.VMEM((2, GROUP, samples, ch2), jnp.bfloat16),
            pltpu.VMEM((samples, ch2), jnp.bfloat16),
            pltpu.SemaphoreType.DMA((2 * UP,)),
            pltpu.SemaphoreType.DMA((cap,)),
            pltpu.SemaphoreType.DMA((2, GROUP)),
        ],
        compiler_params=pltpu.CompilerParams(vmem_limit_bytes=56 * 2**20),
        cost_estimate=pl.CostEstimate(
            flops=2 * rows * ch * (KPRE * width + 2 * UP * ch2),
            bytes_accessed=2 * (w_pre.size + w_up.size + rows * UP * ch2),
            transcendentals=0,
        ),
        name="vocode_used",
    )(target, window, ext, w_pre, biases, snake_params, up_bias, w_up)


def solution(mesh):
    def on_device(features, target, extents, w_pre, biases, snake_params, w_up, up_bias):
        window, ext = exchange(mesh, features, target, extents)
        return vocode(target, window, ext, w_pre, biases, snake_params, w_up, up_bias)

    placed = (
        P(("gen", "voc"), None, None),
        P(("gen", "voc")),
        P(("gen", "voc"), None),
        P(),
        P(),
        P(),
        P(),
        P(),
    )
    return jax.shard_map(
        on_device,
        mesh=mesh,
        in_specs=placed,
        out_specs=P(("gen", "voc"), None, None),
        check_vma=False,
    )
```

```python
import functools
import math

import jax
import jax.numpy as jnp
from jax import lax
from jax.experimental import pallas as pl
from jax.experimental.pallas import tpu as pltpu
from jax.sharding import PartitionSpec as P

UP = 4
KPRE = 7
RIM = 4
GROUP = 8
COL = 256
LANES = 128
MESH = pl.DeviceIdType.MESH
SIN2 = (9.8696029141, -32.4695807761, 42.7253786576, -30.0859046584, 12.9905554979, -3.2727110438)


def f32_dot(a, b):
    return jnp.dot(a, b, preferred_element_type=jnp.float32)


def hot(cond):
    return jnp.where(cond, 1.0, 0.0)


def snake(hidden, alpha, beta):
    turns = hidden * (alpha * (1.0 / math.pi))
    part = turns - jnp.round(turns)
    z = part * part
    poly = jnp.full_like(z, SIN2[-1])
    for coeff in SIN2[-2::-1]:
        poly = poly * z + coeff
    return hidden + (poly * z) * (1.0 / beta)


def exchange_kernel(
    groups, workers, slots,
    feat_ref, target_ref, ext_ref, bias_ref, snake_ref, w_pre_ref,
    win_ref, ext_out_ref, act_ref,
    w_pre, stacked, acts, feat, window, send, got, tail_tx, head_tx, prev_rx, next_rx, back, home,
    s1, r1, s2, r2, s3, r3, w_sem, a_sem,
):
    cap, seg_len, _ = feat_ref.shape
    rows = workers * 8
    width = 2 * RIM * LANES
    half = RIM * LANES
    gen = lax.axis_index("gen")
    voc = lax.axis_index("voc")
    count = groups * workers
    me = gen * workers + voc
    after = lax.rem(me + 1, count)
    before = lax.rem(me + count - 1, count)
    after_id = (lax.div(after, workers), lax.rem(after, workers))
    before_id = (lax.div(before, workers), lax.rem(before, workers))

    load = pltpu.make_async_copy(w_pre_ref, w_pre, w_sem)
    load.start()

    barrier = pltpu.get_barrier_semaphore()
    for d in range(1, workers):
        pl.semaphore_signal(
            barrier, inc=1, device_id=(gen, lax.rem(voc + d, workers)), device_id_type=MESH
        )
    for other in (after_id, before_id):
        pl.semaphore_signal(barrier, inc=1, device_id=other, device_id_type=MESH)

    feat[...] = feat_ref[...].astype(jnp.float32).reshape(cap * seg_len, LANES)

    def frame_of(t):
        return feat[pl.ds(t, cap, stride=seg_len), :].astype(jnp.bfloat16)

    i_c = lax.broadcasted_iota(jnp.int32, (cap, cap), 0)
    i_r = lax.broadcasted_iota(jnp.int32, (cap, cap), 1)
    trow = jnp.broadcast_to(target_ref[...].reshape(1, cap), (cap, cap))
    tcol = jnp.sum(
        jnp.where(i_c == i_r, trow.astype(jnp.float32), 0.0), axis=1, keepdims=True
    ).astype(jnp.int32)
    tcol = jnp.broadcast_to(tcol, (cap, cap))
    used_c = tcol >= 0
    used_r = trow >= 0
    w_c = jnp.where(used_c, lax.div(jnp.maximum(tcol, 0), slots), -1)
    w_r = jnp.where(used_r, lax.div(jnp.maximum(trow, 0), slots), -1)
    same = (w_c == w_r) & used_r
    cnt_r = jnp.sum(hot(same & (i_c < i_r)), axis=0, keepdims=True).astype(jnp.int32)
    cnt_c = jnp.sum(hot(same & (i_r < i_c)), axis=1, keepdims=True).astype(jnp.int32)
    row_r = jnp.where(used_r[:1], w_r[:1] * 8 + cnt_r, -1)
    row_c = jnp.where(used_c[:, :1], w_c[:, :1] * 8 + cnt_c, -1)
    k_c = lax.broadcasted_iota(jnp.int32, (rows, cap), 0)
    k_r = lax.broadcasted_iota(jnp.int32, (cap, rows), 1)
    select = hot(k_c == row_r).astype(jnp.bfloat16)
    select_t = hot(k_r == row_c).astype(jnp.bfloat16)
    earlier = jnp.sum(hot(used_c & (i_c < i_r)), axis=0, keepdims=True).astype(jnp.int32)
    total = jnp.sum(hot(used_c), axis=0, keepdims=True).astype(jnp.int32)
    rank = jnp.where(used_r[:1], earlier, total + i_r[:1] - earlier)
    compact = hot(i_c == rank).astype(jnp.bfloat16)

    slot_c = jnp.where(used_c, lax.rem(jnp.maximum(tcol, 0), slots) + 1, 0)
    slot_b = jnp.broadcast_to(slot_c[:, :1].astype(jnp.float32), (cap, LANES)).astype(jnp.bfloat16)
    rims = list(range(RIM)) + list(range(seg_len - RIM, seg_len))
    parts = jnp.concatenate([frame_of(frame) for frame in rims] + [slot_b], axis=1)
    send[...] = (
        f32_dot(select, parts).reshape(workers, 8, width + LANES).astype(jnp.bfloat16)
    )

    pl.semaphore_wait(barrier, workers + 1)

    def swap(src, dst, send_sem, recv_sem):
        copies = []
        for d in range(1, workers):
            peer = lax.rem(voc + d, workers)
            copy = pltpu.make_async_remote_copy(
                src_ref=src.at[peer],
                dst_ref=dst.at[voc],
                send_sem=send_sem.at[d],
                recv_sem=recv_sem.at[d],
                device_id=(gen, peer),
                device_id_type=MESH,
            )
            copy.start()
            copies.append(copy)
        dst[voc] = src[voc]
        return copies

    copies = swap(send, got, s1, r1)
    picked = hot(i_c == rank)
    ext = []
    for k in range(3):
        row = ext_ref[k : k + 1, :].astype(jnp.float32)
        ext.append(
            jnp.broadcast_to(jnp.sum(picked * row, axis=1, keepdims=True), (cap, LANES))
        )
        ext_out_ref[k] = ext[k]
    for t in range(0, seg_len, 8):
        own = f32_dot(compact, jnp.concatenate([frame_of(t + i) for i in range(8)], axis=1))
        for i in range(8):
            window[RIM + t + i] = own[:, i * LANES : (i + 1) * LANES] * hot(ext[0] > t + i + 0.5)
    inner = seg_len - KPRE + 1
    reach = (KPRE - 1) // 2

    def act_copy(g):
        return pltpu.make_async_copy(acts.at[g], act_ref.at[g], a_sem.at[g])

    def convolve(begin, end):
        @pl.loop(begin, end)
        def _(g):
            at = pl.ds(pl.multiple_of(g * GROUP, GROUP), GROUP)
            for q in range(KPRE):
                stacked[:, q * LANES : (q + 1) * LANES] = (
                    window[RIM + q : RIM + q + inner, at, :]
                    .reshape(inner * GROUP, LANES)
                    .astype(jnp.bfloat16)
                )
            extent = ext_out_ref[0, at, :]
            valid = jnp.concatenate(
                [hot(extent > t + reach + 0.5) for t in range(inner)], axis=0
            )
            valid = jnp.concatenate([valid] * (COL // LANES), axis=1)
            for c in range(0, bias_ref.shape[0], COL):
                cols = slice(c, c + COL)
                hidden = valid * (
                    f32_dot(stacked[...], w_pre[:, cols]) + bias_ref[cols].reshape(1, COL)
                )
                acts[g, :, cols] = snake(
                    hidden, snake_ref[0:1, cols], snake_ref[1:2, cols]
                ).astype(jnp.bfloat16)
            act_copy(g).start()

    groups_here = cap // GROUP
    cuts = (0, groups_here * 3 // 8, groups_here * 5 // 8, groups_here)
    load.wait()
    convolve(cuts[0], cuts[1])
    home_pick = f32_dot(compact, select_t).astype(jnp.bfloat16)
    for copy in copies:
        copy.wait()

    arrived = got[...].astype(jnp.float32).reshape(rows, width + LANES)
    slot_of = arrived[:, width:]
    lane = lax.broadcasted_iota(jnp.int32, (rows, LANES), 1).astype(jnp.float32)
    place = hot(slot_of == lane + 1.0).astype(jnp.bfloat16)
    canon = lax.dot_general(
        place,
        arrived[:, :width].astype(jnp.bfloat16),
        (((0,), (0,)), ((), ())),
        preferred_element_type=jnp.float32,
    )[:slots].astype(jnp.bfloat16)
    head_tx[...] = canon[:, :half]
    tail_tx[...] = canon[:, half:]
    shift = [
        pltpu.make_async_remote_copy(
            src_ref=src, dst_ref=dst, send_sem=s2.at[k], recv_sem=r2.at[k],
            device_id=other, device_id_type=MESH,
        )
        for k, (src, dst, other) in enumerate(
            ((tail_tx, prev_rx, after_id), (head_tx, next_rx, before_id))
        )
    ]
    for copy in shift:
        copy.start()
    held = slot_of > 0.5
    low = slot_of - 1.0 - jnp.where(me == 0, 1.0, 0.0)
    low = jnp.where(low < -0.5, low + float(slots), low)
    high = slot_of - 1.0 + jnp.where(me == count - 1, 1.0, 0.0)
    high = jnp.where(high > slots - 0.5, high - float(slots), high)
    place_prev = hot((low == lane) & held).astype(jnp.bfloat16)[:, :slots]
    place_next = hot((high == lane) & held).astype(jnp.bfloat16)[:, :slots]
    convolve(cuts[1], cuts[2])
    for copy in shift:
        copy.wait()
    back[:, :, :half] = (
        f32_dot(place_prev, prev_rx[...]).reshape(workers, 8, half).astype(jnp.bfloat16)
    )
    back[:, :, half:] = (
        f32_dot(place_next, next_rx[...]).reshape(workers, 8, half).astype(jnp.bfloat16)
    )
    copies = swap(back, home, s3, r3)
    convolve(cuts[2], cuts[3])
    for copy in copies:
        copy.wait()
    homed = home[...].astype(jnp.float32).reshape(rows, width).astype(jnp.bfloat16)
    both = f32_dot(home_pick, homed)
    for t in range(RIM):
        window[t] = both[:, t * LANES : (t + 1) * LANES] * hot(ext[1] > t + seg_len - RIM + 0.5)
        window[RIM + seg_len + t] = both[:, half + t * LANES : half + (t + 1) * LANES] * hot(
            ext[2] > t + 0.5
        )
    span = seg_len + 2 * RIM
    for g in range(cap // GROUP):
        win_ref[g] = (
            window[:, g * GROUP : (g + 1) * GROUP, :]
            .reshape(span * GROUP, LANES)
            .astype(jnp.bfloat16)
        )
    for g in range(groups_here):
        act_copy(g).wait()


def exchange(mesh, features, target, extents, w_pre, biases, snake_params):
    cap, seg_len, width = features.shape
    slots = cap // 2
    workers, groups = mesh.shape["voc"], mesh.shape["gen"]
    span = seg_len + 2 * RIM
    ch = w_pre.shape[1]
    inner = (seg_len - KPRE + 1) * GROUP
    hbm = pl.BlockSpec(memory_space=pl.ANY)
    vmem = pl.BlockSpec(memory_space=pltpu.VMEM)
    bf = jnp.bfloat16
    rim = RIM * width
    return pl.pallas_call(
        functools.partial(exchange_kernel, groups, workers, slots),
        out_shape=[
            jax.ShapeDtypeStruct((cap // GROUP, span * GROUP, width), bf),
            jax.ShapeDtypeStruct((3, cap, LANES), jnp.float32),
            jax.ShapeDtypeStruct((cap // GROUP, inner, ch), bf),
        ],
        in_specs=[vmem] * 5 + [hbm],
        out_specs=[vmem] * 2 + [hbm],
        scratch_shapes=[
            pltpu.VMEM(w_pre.shape, bf),
            pltpu.VMEM((inner, KPRE * width), bf),
            pltpu.VMEM((cap // GROUP, inner, ch), bf),
            pltpu.VMEM((cap * seg_len, width), jnp.float32),
            pltpu.VMEM((span, cap, width), jnp.float32),
            pltpu.VMEM((workers, 8, 2 * rim + LANES), bf),
            pltpu.VMEM((workers, 8, 2 * rim + LANES), bf),
            pltpu.VMEM((slots, rim), bf),
            pltpu.VMEM((slots, rim), bf),
            pltpu.VMEM((slots, rim), bf),
            pltpu.VMEM((slots, rim), bf),
            pltpu.VMEM((workers, 8, 2 * rim), bf),
            pltpu.VMEM((workers, 8, 2 * rim), bf),
            pltpu.SemaphoreType.DMA((workers,)),
            pltpu.SemaphoreType.DMA((workers,)),
            pltpu.SemaphoreType.DMA((2,)),
            pltpu.SemaphoreType.DMA((2,)),
            pltpu.SemaphoreType.DMA((workers,)),
            pltpu.SemaphoreType.DMA((workers,)),
            pltpu.SemaphoreType.DMA,
            pltpu.SemaphoreType.DMA((cap // GROUP,)),
        ],
        compiler_params=pltpu.CompilerParams(
            collective_id=0, has_side_effects=True, vmem_limit_bytes=56 * 2**20
        ),
        name="rim_exchange",
    )(features, target, extents.T, biases, snake_params, w_pre)


def vocode_kernel(
    target_ref, win_ref, ext_ref, w_pre_ref, bias_ref, snake_ref, up_bias_ref, w_up_ref, act_ref,
    out_ref,
    order, taps, stacked, act_even, act_odd, wave32, wave16, zeros, w_sem, z_sem, o_sem, a_sem,
):
    cap = target_ref.shape[0]
    span = win_ref.shape[1] // GROUP
    seg_len = span - 2 * RIM
    first = (KPRE - 1) // 2
    length = span - KPRE + 1
    ch = w_pre_ref.shape[1]
    ch2 = up_bias_ref.shape[0]
    samples = UP * seg_len
    col = COL
    inner = act_ref.shape[1]
    edge = RIM * GROUP

    def centre_tap(r):
        return r + UP // 2

    def side_tap(r):
        return r + 3 * UP // 2 if r < UP // 2 else r - UP // 2

    def load(tap):
        return pltpu.make_async_copy(
            w_up_ref.at[:, pl.ds(tap * ch2, ch2)], taps.at[tap], w_sem.at[tap]
        )

    def act_load(g):
        return pltpu.make_async_copy(
            act_ref.at[g], act_even.at[g, pl.ds(edge, inner)], a_sem.at[g]
        )

    act_load(0).start()
    act_load(1).start()
    for r in range(UP):
        load(centre_tap(r)).start()
        load(side_tap(r)).start()

    def place(i, state):
        a, b = state
        live = jnp.where(target_ref[i] >= 0, 1, 0)
        order[jnp.where(live == 1, a, b)] = i
        return a + live, b - 1 + live

    used, _ = lax.fori_loop(0, cap, place, (0, cap - 1), unroll=True)
    n_groups = lax.div(used + GROUP - 1, GROUP)

    @pl.loop(2, cap // GROUP)
    def _(g):
        act_load(g).start()

    zeros[...] = jnp.zeros_like(zeros)

    def zero_copy(i):
        return pltpu.make_async_copy(zeros, out_ref.at[order[i]], z_sem.at[i])

    @pl.loop(n_groups * GROUP, cap)
    def _(i):
        zero_copy(i).start()

    def frame_mask(g, t):
        at = pl.ds(pl.multiple_of(g * GROUP, GROUP), GROUP)
        if t < RIM:
            return hot(ext_ref[1, at, :] > t + seg_len - RIM + 0.5)
        if t < RIM + seg_len:
            return hot(ext_ref[0, at, :] > t - RIM + 0.5)
        return hot(ext_ref[2, at, :] > t - RIM - seg_len + 0.5)

    @pl.loop(0, n_groups)
    def _(g):
        frames = win_ref[g].astype(jnp.float32)
        last = (length - RIM) * GROUP
        for q in range(KPRE):
            lanes = slice(q * LANES, (q + 1) * LANES)
            low = frames[q * GROUP : q * GROUP + edge]
            high = frames[last + q * GROUP : last + q * GROUP + edge]
            stacked[:, lanes] = jnp.concatenate([low, high], axis=0).astype(jnp.bfloat16)
        outer = list(range(RIM)) + list(range(length - RIM, length))
        valid = jnp.concatenate([frame_mask(g, first + t) for t in outer], axis=0)
        valid = jnp.concatenate([valid] * (col // LANES), axis=1)
        act_load(g).wait()
        for c in range(0, ch, col):
            cols = slice(c, c + col)
            hidden = valid * (
                f32_dot(stacked[...], w_pre_ref[:, cols]) + bias_ref[cols].reshape(1, col)
            )
            act = snake(hidden, snake_ref[0:1, cols], snake_ref[1:2, cols])
            act_even[g, :edge, cols] = act[:edge].astype(jnp.bfloat16)
            act_even[g, edge + inner :, cols] = act[edge:].astype(jnp.bfloat16)
            middle = act_even[g, edge : edge + inner, cols].astype(jnp.float32)
            act_odd[g, :, cols] = jnp.concatenate(
                [act[GROUP:edge], middle, act[edge : 2 * edge - GROUP]], axis=0
            ).astype(jnp.bfloat16)

    @pl.loop(n_groups, cap // GROUP)
    def _(g):
        act_load(g).wait()

    for r in range(UP):
        load(centre_tap(r)).wait()
        load(side_tap(r)).wait()

    def wave_copy(g, slot, k):
        return pltpu.make_async_copy(
            wave16.at[slot, k], out_ref.at[order[g * GROUP + k]], o_sem.at[slot, k]
        )

    rows = seg_len * GROUP
    pitch = samples + 1

    @pl.loop(0, n_groups)
    def _(g):
        slot = lax.rem(g, 2)

        @pl.when(g >= 2)
        def _():
            for k in range(GROUP):
                wave_copy(g - 2, slot, k).wait()

        for c in range(0, ch2, col):
            cols = slice(c, c + col)
            bias = up_bias_ref[cols].reshape(1, col)
            for r in range(UP):
                side_at = 0 if r < UP // 2 else 2 * GROUP
                total = f32_dot(act_odd[g], taps[centre_tap(r), :, cols]) + f32_dot(
                    act_even[g, side_at : side_at + rows, :], taps[side_tap(r), :, cols]
                )
                total = total + bias
                for j in range(seg_len):
                    keep = frame_mask(g, RIM + j)
                    for h in range(col // LANES):
                        block = (c // LANES + h) * GROUP
                        wave32[pl.ds(block * pitch + UP * j + r, GROUP, stride=pitch), :] = (
                            keep * total[j * GROUP : (j + 1) * GROUP, h * LANES : (h + 1) * LANES]
                        )
            for h in range(c // LANES, (c + col) // LANES):
                for k in range(GROUP):
                    start = (h * GROUP + k) * pitch
                    wave16[slot, k, :, h * LANES : (h + 1) * LANES] = wave32[
                        start : start + samples, :
                    ].astype(jnp.bfloat16)

        for k in range(GROUP):
            wave_copy(g, slot, k).start()

    for lag in (2, 1):

        @pl.when(n_groups >= lag)
        def _():
            g = n_groups - lag
            for k in range(GROUP):
                wave_copy(g, lax.rem(g, 2), k).wait()

    @pl.loop(n_groups * GROUP, cap)
    def _(i):
        zero_copy(i).wait()


def vocode(target, window, ext, acts, w_pre, biases, snake_params, w_up, up_bias):
    cap, width = target.shape[0], window.shape[2]
    span = window.shape[1] // GROUP
    seg_len = span - 2 * RIM
    ch, ch2 = w_pre.shape[1], up_bias.shape[0]
    length = span - KPRE + 1
    groups = cap // GROUP
    samples = UP * seg_len
    vmem = pl.BlockSpec(memory_space=pltpu.VMEM)
    hbm = pl.BlockSpec(memory_space=pl.ANY)
    rows = cap * seg_len
    return pl.pallas_call(
        vocode_kernel,
        out_shape=jax.ShapeDtypeStruct((cap, samples, ch2), jnp.bfloat16),
        in_specs=[pl.BlockSpec(memory_space=pltpu.SMEM)] + [vmem] * 6 + [hbm] * 2,
        out_specs=hbm,
        scratch_shapes=[
            pltpu.SMEM((cap,), jnp.int32),
            pltpu.VMEM((2 * UP, ch, ch2), jnp.bfloat16),
            pltpu.VMEM((2 * RIM * GROUP, KPRE * width), jnp.bfloat16),
            pltpu.VMEM((groups, length * GROUP, ch), jnp.bfloat16),
            pltpu.VMEM((groups, seg_len * GROUP, ch), jnp.bfloat16),
            pltpu.VMEM((ch2 // LANES * GROUP * (samples + 1), LANES), jnp.float32),
            pltpu.VMEM((2, GROUP, samples, ch2), jnp.bfloat16),
            pltpu.VMEM((samples, ch2), jnp.bfloat16),
            pltpu.SemaphoreType.DMA((2 * UP,)),
            pltpu.SemaphoreType.DMA((cap,)),
            pltpu.SemaphoreType.DMA((2, GROUP)),
            pltpu.SemaphoreType.DMA((groups,)),
        ],
        compiler_params=pltpu.CompilerParams(vmem_limit_bytes=56 * 2**20),
        cost_estimate=pl.CostEstimate(
            flops=2 * rows * ch * (KPRE * width + 2 * UP * ch2),
            bytes_accessed=2 * (w_pre.size + w_up.size + rows * UP * ch2),
            transcendentals=0,
        ),
        name="vocode_used",
    )(target, window, ext, w_pre, biases, snake_params, up_bias, w_up, acts)


def solution(mesh):
    def on_device(features, target, extents, w_pre, biases, snake_params, w_up, up_bias):
        window, ext, acts = exchange(
            mesh, features, target, extents, w_pre, biases, snake_params
        )
        return vocode(target, window, ext, acts, w_pre, biases, snake_params, w_up, up_bias)

    placed = (
        P(("gen", "voc"), None, None),
        P(("gen", "voc")),
        P(("gen", "voc"), None),
        P(),
        P(),
        P(),
        P(),
        P(),
    )
    return jax.shard_map(
        on_device,
        mesh=mesh,
        in_specs=placed,
        out_specs=P(("gen", "voc"), None, None),
        check_vma=False,
    )
```

```python
import functools
import math

import jax
import jax.numpy as jnp
from jax import lax
from jax.experimental import pallas as pl
from jax.experimental.pallas import tpu as pltpu
from jax.sharding import PartitionSpec as P

UP = 4
KPRE = 7
RIM = 4
GROUP = 8
COL = 256
LANES = 128
MESH = pl.DeviceIdType.MESH
SIN2 = (9.8696029141, -32.4695807761, 42.7253786576, -30.0859046584, 12.9905554979, -3.2727110438)


def f32_dot(a, b):
    return jnp.dot(a, b, preferred_element_type=jnp.float32)


def hot(cond):
    return jnp.where(cond, 1.0, 0.0)


def snake(hidden, alpha, beta):
    turns = hidden * (alpha * (1.0 / math.pi))
    part = turns - jnp.round(turns)
    z = part * part
    poly = jnp.full_like(z, SIN2[-1])
    for coeff in SIN2[-2::-1]:
        poly = poly * z + coeff
    return hidden + (poly * z) * (1.0 / beta)


def exchange_kernel(
    groups, workers, slots,
    feat_in, target_in, ext_in, bias_in, snake_in, up_bias_in, w_pre_ref, w_up_ref,
    win_ref, ext_out_ref, act_ref, target_ref, bias_ref, snake_ref, up_bias_ref, w_pre, taps,
    feat_ref, ext_ref, i_sem, stacked, acts, feat, window, send, got, tail_tx, head_tx, prev_rx, next_rx, back, home,
    s1, r1, s2, r2, s3, r3, w_sem, t_sem, a_sem,
):
    cap, seg_len, _ = feat_ref.shape
    rows = workers * 8
    width = 2 * RIM * LANES
    half = RIM * LANES
    gen = lax.axis_index("gen")
    voc = lax.axis_index("voc")
    count = groups * workers
    me = gen * workers + voc
    after = lax.rem(me + 1, count)
    before = lax.rem(me + count - 1, count)
    after_id = (lax.div(after, workers), lax.rem(after, workers))
    before_id = (lax.div(before, workers), lax.rem(before, workers))

    inputs = [
        pltpu.make_async_copy(src, dst, i_sem.at[k])
        for k, (src, dst) in enumerate(
            (
                (target_in, target_ref),
                (feat_in, feat_ref),
                (ext_in, ext_ref),
                (bias_in, bias_ref),
                (snake_in, snake_ref),
                (up_bias_in, up_bias_ref),
            )
        )
    ]
    for copy in inputs:
        copy.start()
    load = pltpu.make_async_copy(w_pre_ref, w_pre, w_sem)
    load.start()
    ch2 = taps.shape[2]
    tap_loads = [
        pltpu.make_async_copy(
            w_up_ref.at[:, pl.ds(tap * ch2, ch2)], taps.at[tap], t_sem.at[tap]
        )
        for tap in range(2 * UP)
    ]
    for tap_load in tap_loads:
        tap_load.start()

    barrier = pltpu.get_barrier_semaphore()
    for d in range(1, workers):
        pl.semaphore_signal(
            barrier, inc=1, device_id=(gen, lax.rem(voc + d, workers)), device_id_type=MESH
        )
    for other in (after_id, before_id):
        pl.semaphore_signal(barrier, inc=1, device_id=other, device_id_type=MESH)

    for copy in inputs:
        copy.wait()
    feat[...] = feat_ref[...].astype(jnp.float32).reshape(cap * seg_len, LANES)

    def frame_of(t):
        return feat[pl.ds(t, cap, stride=seg_len), :].astype(jnp.bfloat16)

    i_c = lax.broadcasted_iota(jnp.int32, (cap, cap), 0)
    i_r = lax.broadcasted_iota(jnp.int32, (cap, cap), 1)
    trow = jnp.broadcast_to(target_ref[...].reshape(1, cap), (cap, cap))
    tcol = jnp.sum(
        jnp.where(i_c == i_r, trow.astype(jnp.float32), 0.0), axis=1, keepdims=True
    ).astype(jnp.int32)
    tcol = jnp.broadcast_to(tcol, (cap, cap))
    used_c = tcol >= 0
    used_r = trow >= 0
    w_c = jnp.where(used_c, lax.div(jnp.maximum(tcol, 0), slots), -1)
    w_r = jnp.where(used_r, lax.div(jnp.maximum(trow, 0), slots), -1)
    same = (w_c == w_r) & used_r
    cnt_r = jnp.sum(hot(same & (i_c < i_r)), axis=0, keepdims=True).astype(jnp.int32)
    cnt_c = jnp.sum(hot(same & (i_r < i_c)), axis=1, keepdims=True).astype(jnp.int32)
    row_r = jnp.where(used_r[:1], w_r[:1] * 8 + cnt_r, -1)
    row_c = jnp.where(used_c[:, :1], w_c[:, :1] * 8 + cnt_c, -1)
    k_c = lax.broadcasted_iota(jnp.int32, (rows, cap), 0)
    k_r = lax.broadcasted_iota(jnp.int32, (cap, rows), 1)
    select = hot(k_c == row_r).astype(jnp.bfloat16)
    select_t = hot(k_r == row_c).astype(jnp.bfloat16)
    earlier = jnp.sum(hot(used_c & (i_c < i_r)), axis=0, keepdims=True).astype(jnp.int32)
    total = jnp.sum(hot(used_c), axis=0, keepdims=True).astype(jnp.int32)
    rank = jnp.where(used_r[:1], earlier, total + i_r[:1] - earlier)
    compact = hot(i_c == rank).astype(jnp.bfloat16)

    slot_c = jnp.where(used_c, lax.rem(jnp.maximum(tcol, 0), slots) + 1, 0)
    slot_b = jnp.broadcast_to(slot_c[:, :1].astype(jnp.float32), (cap, LANES)).astype(jnp.bfloat16)
    rims = list(range(RIM)) + list(range(seg_len - RIM, seg_len))
    parts = jnp.concatenate([frame_of(frame) for frame in rims] + [slot_b], axis=1)
    send[...] = (
        f32_dot(select, parts).reshape(workers, 8, width + LANES).astype(jnp.bfloat16)
    )

    pl.semaphore_wait(barrier, workers + 1)

    def swap(src, dst, send_sem, recv_sem):
        copies = []
        for d in range(1, workers):
            peer = lax.rem(voc + d, workers)
            copy = pltpu.make_async_remote_copy(
                src_ref=src.at[peer],
                dst_ref=dst.at[voc],
                send_sem=send_sem.at[d],
                recv_sem=recv_sem.at[d],
                device_id=(gen, peer),
                device_id_type=MESH,
            )
            copy.start()
            copies.append(copy)
        dst[voc] = src[voc]
        return copies

    copies = swap(send, got, s1, r1)
    picked = hot(i_c == rank)
    ext = []
    for k in range(3):
        row = ext_ref[k : k + 1, :].astype(jnp.float32)
        ext.append(
            jnp.broadcast_to(jnp.sum(picked * row, axis=1, keepdims=True), (cap, LANES))
        )
        ext_out_ref[k] = ext[k]
    for t in range(0, seg_len, 8):
        own = f32_dot(compact, jnp.concatenate([frame_of(t + i) for i in range(8)], axis=1))
        for i in range(8):
            window[RIM + t + i] = own[:, i * LANES : (i + 1) * LANES] * hot(ext[0] > t + i + 0.5)
    inner = seg_len - KPRE + 1
    reach = (KPRE - 1) // 2

    def act_copy(g):
        return pltpu.make_async_copy(acts.at[g], act_ref.at[g], a_sem.at[g])

    def convolve(begin, end):
        @pl.loop(begin, end)
        def _(g):
            at = pl.ds(pl.multiple_of(g * GROUP, GROUP), GROUP)
            for q in range(KPRE):
                stacked[:, q * LANES : (q + 1) * LANES] = (
                    window[RIM + q : RIM + q + inner, at, :]
                    .reshape(inner * GROUP, LANES)
                    .astype(jnp.bfloat16)
                )
            extent = ext_out_ref[0, at, :]
            valid = jnp.concatenate(
                [hot(extent > t + reach + 0.5) for t in range(inner)], axis=0
            )
            valid = jnp.concatenate([valid] * (COL // LANES), axis=1)
            for c in range(0, bias_ref.shape[0], COL):
                cols = slice(c, c + COL)
                hidden = valid * (
                    f32_dot(stacked[...], w_pre[:, cols]) + bias_ref[cols].reshape(1, COL)
                )
                acts[g, :, cols] = snake(
                    hidden, snake_ref[0:1, cols], snake_ref[1:2, cols]
                ).astype(jnp.bfloat16)
            act_copy(g).start()

    groups_here = cap // GROUP
    cuts = (0, groups_here * 3 // 8, groups_here * 5 // 8, groups_here)
    load.wait()
    convolve(cuts[0], cuts[1])
    home_pick = f32_dot(compact, select_t).astype(jnp.bfloat16)
    for copy in copies:
        copy.wait()

    arrived = got[...].astype(jnp.float32).reshape(rows, width + LANES)
    slot_of = arrived[:, width:]
    lane = lax.broadcasted_iota(jnp.int32, (rows, LANES), 1).astype(jnp.float32)
    place = hot(slot_of == lane + 1.0).astype(jnp.bfloat16)
    canon = lax.dot_general(
        place,
        arrived[:, :width].astype(jnp.bfloat16),
        (((0,), (0,)), ((), ())),
        preferred_element_type=jnp.float32,
    )[:slots].astype(jnp.bfloat16)
    head_tx[...] = canon[:, :half]
    tail_tx[...] = canon[:, half:]
    shift = [
        pltpu.make_async_remote_copy(
            src_ref=src, dst_ref=dst, send_sem=s2.at[k], recv_sem=r2.at[k],
            device_id=other, device_id_type=MESH,
        )
        for k, (src, dst, other) in enumerate(
            ((tail_tx, prev_rx, after_id), (head_tx, next_rx, before_id))
        )
    ]
    for copy in shift:
        copy.start()
    held = slot_of > 0.5
    low = slot_of - 1.0 - jnp.where(me == 0, 1.0, 0.0)
    low = jnp.where(low < -0.5, low + float(slots), low)
    high = slot_of - 1.0 + jnp.where(me == count - 1, 1.0, 0.0)
    high = jnp.where(high > slots - 0.5, high - float(slots), high)
    place_prev = hot((low == lane) & held).astype(jnp.bfloat16)[:, :slots]
    place_next = hot((high == lane) & held).astype(jnp.bfloat16)[:, :slots]
    convolve(cuts[1], cuts[2])
    for copy in shift:
        copy.wait()
    back[:, :, :half] = (
        f32_dot(place_prev, prev_rx[...]).reshape(workers, 8, half).astype(jnp.bfloat16)
    )
    back[:, :, half:] = (
        f32_dot(place_next, next_rx[...]).reshape(workers, 8, half).astype(jnp.bfloat16)
    )
    copies = swap(back, home, s3, r3)
    convolve(cuts[2], cuts[3])
    for copy in copies:
        copy.wait()
    homed = home[...].astype(jnp.float32).reshape(rows, width).astype(jnp.bfloat16)
    both = f32_dot(home_pick, homed)
    for t in range(RIM):
        window[t] = both[:, t * LANES : (t + 1) * LANES] * hot(ext[1] > t + seg_len - RIM + 0.5)
        window[RIM + seg_len + t] = both[:, half + t * LANES : half + (t + 1) * LANES] * hot(
            ext[2] > t + 0.5
        )
    span = seg_len + 2 * RIM
    for g in range(cap // GROUP):
        win_ref[g] = (
            window[:, g * GROUP : (g + 1) * GROUP, :]
            .reshape(span * GROUP, LANES)
            .astype(jnp.bfloat16)
        )
    for g in range(groups_here):
        act_copy(g).wait()
    for tap_load in tap_loads:
        tap_load.wait()


def exchange(mesh, features, target, extents, w_pre, biases, snake_params, w_up, up_bias):
    cap, seg_len, width = features.shape
    slots = cap // 2
    workers, groups = mesh.shape["voc"], mesh.shape["gen"]
    span = seg_len + 2 * RIM
    ch = w_pre.shape[1]
    inner = (seg_len - KPRE + 1) * GROUP
    hbm = pl.BlockSpec(memory_space=pl.ANY)
    vmem = pl.BlockSpec(memory_space=pltpu.VMEM)
    bf = jnp.bfloat16
    rim = RIM * width
    return pl.pallas_call(
        functools.partial(exchange_kernel, groups, workers, slots),
        out_shape=[
            jax.ShapeDtypeStruct((cap // GROUP, span * GROUP, width), bf),
            jax.ShapeDtypeStruct((3, cap, LANES), jnp.float32),
            jax.ShapeDtypeStruct((cap // GROUP, inner, ch), bf),
            jax.ShapeDtypeStruct(target.shape, jnp.int32),
            jax.ShapeDtypeStruct(biases.shape, jnp.float32),
            jax.ShapeDtypeStruct(snake_params.shape, jnp.float32),
            jax.ShapeDtypeStruct(up_bias.shape, jnp.float32),
            jax.ShapeDtypeStruct(w_pre.shape, bf),
            jax.ShapeDtypeStruct((2 * UP, ch, w_up.shape[1] // (2 * UP)), bf),
        ],
        in_specs=[pl.BlockSpec(memory_space=pltpu.HBM)] * 8,
        out_specs=[vmem] * 2 + [hbm] + [vmem] * 6,
        scratch_shapes=[
            pltpu.VMEM(features.shape, bf),
            pltpu.VMEM((3, cap), jnp.int32),
            pltpu.SemaphoreType.DMA((6,)),
            pltpu.VMEM((inner, KPRE * width), bf),
            pltpu.VMEM((cap // GROUP, inner, ch), bf),
            pltpu.VMEM((cap * seg_len, width), jnp.float32),
            pltpu.VMEM((span, cap, width), jnp.float32),
            pltpu.VMEM((workers, 8, 2 * rim + LANES), bf),
            pltpu.VMEM((workers, 8, 2 * rim + LANES), bf),
            pltpu.VMEM((slots, rim), bf),
            pltpu.VMEM((slots, rim), bf),
            pltpu.VMEM((slots, rim), bf),
            pltpu.VMEM((slots, rim), bf),
            pltpu.VMEM((workers, 8, 2 * rim), bf),
            pltpu.VMEM((workers, 8, 2 * rim), bf),
            pltpu.SemaphoreType.DMA((workers,)),
            pltpu.SemaphoreType.DMA((workers,)),
            pltpu.SemaphoreType.DMA((2,)),
            pltpu.SemaphoreType.DMA((2,)),
            pltpu.SemaphoreType.DMA((workers,)),
            pltpu.SemaphoreType.DMA((workers,)),
            pltpu.SemaphoreType.DMA,
            pltpu.SemaphoreType.DMA((2 * UP,)),
            pltpu.SemaphoreType.DMA((cap // GROUP,)),
        ],
        compiler_params=pltpu.CompilerParams(
            collective_id=0, has_side_effects=True, vmem_limit_bytes=14 * 2**20
        ),
        name="rim_exchange",
    )(
        *(
            pltpu.with_memory_space_constraint(value, pltpu.HBM)
            for value in (
                features, target, extents.T, biases, snake_params, up_bias, w_pre, w_up
            )
        )
    )


def vocode_kernel(
    target_ref, win_ref, ext_ref, w_pre_ref, bias_ref, snake_ref, up_bias_ref, taps, act_ref,
    out_ref,
    order, stacked, act_even, act_odd, wave32, wave16, zeros, z_sem, o_sem, a_sem,
):
    cap = target_ref.shape[0]
    span = win_ref.shape[1] // GROUP
    seg_len = span - 2 * RIM
    first = (KPRE - 1) // 2
    length = span - KPRE + 1
    ch = w_pre_ref.shape[1]
    ch2 = up_bias_ref.shape[0]
    samples = UP * seg_len
    col = COL
    inner = act_ref.shape[1]
    edge = RIM * GROUP

    def centre_tap(r):
        return r + UP // 2

    def side_tap(r):
        return r + 3 * UP // 2 if r < UP // 2 else r - UP // 2

    def act_load(g):
        return pltpu.make_async_copy(
            act_ref.at[g], act_even.at[g, pl.ds(edge, inner)], a_sem.at[g]
        )

    act_load(0).start()
    act_load(1).start()
    def place(i, state):
        a, b = state
        live = jnp.where(target_ref[i] >= 0, 1, 0)
        order[jnp.where(live == 1, a, b)] = i
        return a + live, b - 1 + live

    used, _ = lax.fori_loop(0, cap, place, (0, cap - 1), unroll=True)
    n_groups = lax.div(used + GROUP - 1, GROUP)

    @pl.loop(2, cap // GROUP)
    def _(g):
        act_load(g).start()

    zeros[...] = jnp.zeros_like(zeros)

    def zero_copy(i):
        return pltpu.make_async_copy(zeros, out_ref.at[order[i]], z_sem.at[i])

    @pl.loop(n_groups * GROUP, cap)
    def _(i):
        zero_copy(i).start()

    def frame_mask(g, t):
        at = pl.ds(pl.multiple_of(g * GROUP, GROUP), GROUP)
        if t < RIM:
            return hot(ext_ref[1, at, :] > t + seg_len - RIM + 0.5)
        if t < RIM + seg_len:
            return hot(ext_ref[0, at, :] > t - RIM + 0.5)
        return hot(ext_ref[2, at, :] > t - RIM - seg_len + 0.5)

    @pl.loop(0, n_groups)
    def _(g):
        frames = win_ref[g].astype(jnp.float32)
        last = (length - RIM) * GROUP
        for q in range(KPRE):
            lanes = slice(q * LANES, (q + 1) * LANES)
            low = frames[q * GROUP : q * GROUP + edge]
            high = frames[last + q * GROUP : last + q * GROUP + edge]
            stacked[:, lanes] = jnp.concatenate([low, high], axis=0).astype(jnp.bfloat16)
        outer = list(range(RIM)) + list(range(length - RIM, length))
        valid = jnp.concatenate([frame_mask(g, first + t) for t in outer], axis=0)
        valid = jnp.concatenate([valid] * (col // LANES), axis=1)
        act_load(g).wait()
        for c in range(0, ch, col):
            cols = slice(c, c + col)
            hidden = valid * (
                f32_dot(stacked[...], w_pre_ref[:, cols]) + bias_ref[cols].reshape(1, col)
            )
            act = snake(hidden, snake_ref[0:1, cols], snake_ref[1:2, cols])
            act_even[g, :edge, cols] = act[:edge].astype(jnp.bfloat16)
            act_even[g, edge + inner :, cols] = act[edge:].astype(jnp.bfloat16)
            middle = act_even[g, edge : edge + inner, cols].astype(jnp.float32)
            act_odd[g, :, cols] = jnp.concatenate(
                [act[GROUP:edge], middle, act[edge : 2 * edge - GROUP]], axis=0
            ).astype(jnp.bfloat16)

    @pl.loop(n_groups, cap // GROUP)
    def _(g):
        act_load(g).wait()

    def wave_copy(g, slot, k):
        return pltpu.make_async_copy(
            wave16.at[slot, k], out_ref.at[order[g * GROUP + k]], o_sem.at[slot, k]
        )

    rows = seg_len * GROUP
    pitch = samples + 1

    @pl.loop(0, n_groups)
    def _(g):
        slot = lax.rem(g, 2)

        @pl.when(g >= 2)
        def _():
            for k in range(GROUP):
                wave_copy(g - 2, slot, k).wait()

        for c in range(0, ch2, col):
            cols = slice(c, c + col)
            bias = up_bias_ref[cols].reshape(1, col)
            for r in range(UP):
                side_at = 0 if r < UP // 2 else 2 * GROUP
                total = f32_dot(act_odd[g], taps[centre_tap(r), :, cols]) + f32_dot(
                    act_even[g, side_at : side_at + rows, :], taps[side_tap(r), :, cols]
                )
                total = total + bias
                for j in range(seg_len):
                    keep = frame_mask(g, RIM + j)
                    for h in range(col // LANES):
                        block = (c // LANES + h) * GROUP
                        wave32[pl.ds(block * pitch + UP * j + r, GROUP, stride=pitch), :] = (
                            keep * total[j * GROUP : (j + 1) * GROUP, h * LANES : (h + 1) * LANES]
                        )
            for h in range(c // LANES, (c + col) // LANES):
                for k in range(GROUP):
                    start = (h * GROUP + k) * pitch
                    wave16[slot, k, :, h * LANES : (h + 1) * LANES] = wave32[
                        start : start + samples, :
                    ].astype(jnp.bfloat16)

        for k in range(GROUP):
            wave_copy(g, slot, k).start()

    for lag in (2, 1):

        @pl.when(n_groups >= lag)
        def _():
            g = n_groups - lag
            for k in range(GROUP):
                wave_copy(g, lax.rem(g, 2), k).wait()

    @pl.loop(n_groups * GROUP, cap)
    def _(i):
        zero_copy(i).wait()


def vocode(target, window, ext, acts, w_pre, biases, snake_params, taps, up_bias):
    cap, width = target.shape[0], window.shape[2]
    span = window.shape[1] // GROUP
    seg_len = span - 2 * RIM
    ch, ch2 = w_pre.shape[1], up_bias.shape[0]
    length = span - KPRE + 1
    groups = cap // GROUP
    samples = UP * seg_len
    vmem = pl.BlockSpec(memory_space=pltpu.VMEM)
    hbm = pl.BlockSpec(memory_space=pl.ANY)
    rows = cap * seg_len
    return pl.pallas_call(
        vocode_kernel,
        out_shape=jax.ShapeDtypeStruct((cap, samples, ch2), jnp.bfloat16),
        in_specs=[pl.BlockSpec(memory_space=pltpu.SMEM)] + [vmem] * 7 + [hbm],
        out_specs=hbm,
        scratch_shapes=[
            pltpu.SMEM((cap,), jnp.int32),
            pltpu.VMEM((2 * RIM * GROUP, KPRE * width), jnp.bfloat16),
            pltpu.VMEM((groups, length * GROUP, ch), jnp.bfloat16),
            pltpu.VMEM((groups, seg_len * GROUP, ch), jnp.bfloat16),
            pltpu.VMEM((ch2 // LANES * GROUP * (samples + 1), LANES), jnp.float32),
            pltpu.VMEM((2, GROUP, samples, ch2), jnp.bfloat16),
            pltpu.VMEM((samples, ch2), jnp.bfloat16),
            pltpu.SemaphoreType.DMA((cap,)),
            pltpu.SemaphoreType.DMA((2, GROUP)),
            pltpu.SemaphoreType.DMA((groups,)),
        ],
        compiler_params=pltpu.CompilerParams(vmem_limit_bytes=22 * 2**20),
        cost_estimate=pl.CostEstimate(
            flops=2 * rows * ch * (KPRE * width + 2 * UP * ch2),
            bytes_accessed=2 * (w_pre.size + taps.size + rows * UP * ch2),
            transcendentals=0,
        ),
        name="vocode_used",
    )(target, window, ext, w_pre, biases, snake_params, up_bias, taps, acts)


def solution(mesh):
    def on_device(features, target, extents, w_pre, biases, snake_params, w_up, up_bias):
        window, ext, acts, target, biases, snake_params, up_bias, w_near, taps = exchange(
            mesh, features, target, extents, w_pre, biases, snake_params, w_up, up_bias
        )
        return vocode(target, window, ext, acts, w_near, biases, snake_params, taps, up_bias)

    placed = (
        P(("gen", "voc"), None, None),
        P(("gen", "voc")),
        P(("gen", "voc"), None),
        P(),
        P(),
        P(),
        P(),
        P(),
    )
    return jax.shard_map(
        on_device,
        mesh=mesh,
        in_specs=placed,
        out_specs=P(("gen", "voc"), None, None),
        check_vma=False,
    )
```

```python
import functools
import math

import jax
import jax.numpy as jnp
from jax import lax
from jax.experimental import pallas as pl
from jax.experimental.pallas import tpu as pltpu
from jax.sharding import PartitionSpec as P

UP = 4
KPRE = 7
RIM = 4
GROUP = 8
COL = 256
LANES = 128
MESH = pl.DeviceIdType.MESH
SIN2 = (9.8696029141, -32.4695807761, 42.7253786576, -30.0859046584, 12.9905554979, -3.2727110438)


def f32_dot(a, b):
    return jnp.dot(a, b, preferred_element_type=jnp.float32)


def hot(cond):
    return jnp.where(cond, 1.0, 0.0)


def snake(hidden, alpha, beta):
    turns = hidden * (alpha * (1.0 / math.pi))
    part = turns - jnp.round(turns)
    z = part * part
    poly = jnp.full_like(z, SIN2[-1])
    for coeff in SIN2[-2::-1]:
        poly = poly * z + coeff
    return hidden + (poly * z) * (1.0 / beta)


def exchange_kernel(
    groups, workers, slots,
    feat_in, target_in, ext_in, bias_in, snake_in, up_bias_in, w_pre_ref, w_up_ref,
    win_ref, ext_out_ref, act_ref, target_ref, bias_ref, snake_ref, up_bias_ref, w_pre, taps,
    feat_ref, ext_ref, i_sem, stacked, acts, feat, window, send, got, tail_tx, head_tx, prev_rx, next_rx, back, home,
    s1, r1, s2, r2, s3, r3, w_sem, t_sem, a_sem,
):
    cap, seg_len, _ = feat_ref.shape
    rows = workers * 8
    width = 2 * RIM * LANES
    half = RIM * LANES
    gen = lax.axis_index("gen")
    voc = lax.axis_index("voc")
    count = groups * workers
    me = gen * workers + voc
    after = lax.rem(me + 1, count)
    before = lax.rem(me + count - 1, count)
    after_id = (lax.div(after, workers), lax.rem(after, workers))
    before_id = (lax.div(before, workers), lax.rem(before, workers))

    inputs = [
        pltpu.make_async_copy(src, dst, i_sem.at[k])
        for k, (src, dst) in enumerate(
            (
                (target_in, target_ref),
                (feat_in, feat_ref),
                (ext_in, ext_ref),
                (bias_in, bias_ref),
                (snake_in, snake_ref),
                (up_bias_in, up_bias_ref),
            )
        )
    ]
    for copy in inputs:
        copy.start()
    load = pltpu.make_async_copy(w_pre_ref, w_pre, w_sem)
    load.start()
    ch2 = taps.shape[2]
    tap_loads = [
        pltpu.make_async_copy(
            w_up_ref.at[:, pl.ds(tap * ch2, ch2)], taps.at[tap], t_sem.at[tap]
        )
        for tap in range(2 * UP)
    ]

    barrier = pltpu.get_barrier_semaphore()
    for d in range(1, workers):
        pl.semaphore_signal(
            barrier, inc=1, device_id=(gen, lax.rem(voc + d, workers)), device_id_type=MESH
        )
    for other in (after_id, before_id):
        pl.semaphore_signal(barrier, inc=1, device_id=other, device_id_type=MESH)

    for copy in inputs:
        copy.wait()
    feat[...] = feat_ref[...].astype(jnp.float32).reshape(cap * seg_len, LANES)

    def frame_of(t):
        return feat[pl.ds(t, cap, stride=seg_len), :].astype(jnp.bfloat16)

    i_c = lax.broadcasted_iota(jnp.int32, (cap, cap), 0)
    i_r = lax.broadcasted_iota(jnp.int32, (cap, cap), 1)
    trow = jnp.broadcast_to(target_ref[...].reshape(1, cap), (cap, cap))
    tcol = jnp.sum(
        jnp.where(i_c == i_r, trow.astype(jnp.float32), 0.0), axis=1, keepdims=True
    ).astype(jnp.int32)
    tcol = jnp.broadcast_to(tcol, (cap, cap))
    used_c = tcol >= 0
    used_r = trow >= 0
    w_c = jnp.where(used_c, lax.div(jnp.maximum(tcol, 0), slots), -1)
    w_r = jnp.where(used_r, lax.div(jnp.maximum(trow, 0), slots), -1)
    same = (w_c == w_r) & used_r
    cnt_r = jnp.sum(hot(same & (i_c < i_r)), axis=0, keepdims=True).astype(jnp.int32)
    cnt_c = jnp.sum(hot(same & (i_r < i_c)), axis=1, keepdims=True).astype(jnp.int32)
    row_r = jnp.where(used_r[:1], w_r[:1] * 8 + cnt_r, -1)
    row_c = jnp.where(used_c[:, :1], w_c[:, :1] * 8 + cnt_c, -1)
    k_c = lax.broadcasted_iota(jnp.int32, (rows, cap), 0)
    k_r = lax.broadcasted_iota(jnp.int32, (cap, rows), 1)
    select = hot(k_c == row_r).astype(jnp.bfloat16)
    select_t = hot(k_r == row_c).astype(jnp.bfloat16)
    earlier = jnp.sum(hot(used_c & (i_c < i_r)), axis=0, keepdims=True).astype(jnp.int32)
    total = jnp.sum(hot(used_c), axis=0, keepdims=True).astype(jnp.int32)
    rank = jnp.where(used_r[:1], earlier, total + i_r[:1] - earlier)
    compact = hot(i_c == rank).astype(jnp.bfloat16)

    slot_c = jnp.where(used_c, lax.rem(jnp.maximum(tcol, 0), slots) + 1, 0)
    slot_b = jnp.broadcast_to(slot_c[:, :1].astype(jnp.float32), (cap, LANES)).astype(jnp.bfloat16)
    rims = list(range(RIM)) + list(range(seg_len - RIM, seg_len))
    parts = jnp.concatenate([frame_of(frame) for frame in rims] + [slot_b], axis=1)
    send[...] = (
        f32_dot(select, parts).reshape(workers, 8, width + LANES).astype(jnp.bfloat16)
    )

    pl.semaphore_wait(barrier, workers + 1)

    def swap(src, dst, send_sem, recv_sem):
        copies = []
        for d in range(1, workers):
            peer = lax.rem(voc + d, workers)
            copy = pltpu.make_async_remote_copy(
                src_ref=src.at[peer],
                dst_ref=dst.at[voc],
                send_sem=send_sem.at[d],
                recv_sem=recv_sem.at[d],
                device_id=(gen, peer),
                device_id_type=MESH,
            )
            copy.start()
            copies.append(copy)
        dst[voc] = src[voc]
        return copies

    copies = swap(send, got, s1, r1)
    picked = hot(i_c == rank)
    ext = []
    for k in range(3):
        row = ext_ref[k : k + 1, :].astype(jnp.float32)
        ext.append(
            jnp.broadcast_to(jnp.sum(picked * row, axis=1, keepdims=True), (cap, LANES))
        )
        ext_out_ref[k] = ext[k]
    for t in range(0, seg_len, 8):
        own = f32_dot(compact, jnp.concatenate([frame_of(t + i) for i in range(8)], axis=1))
        for i in range(8):
            window[RIM + t + i] = own[:, i * LANES : (i + 1) * LANES] * hot(ext[0] > t + i + 0.5)
    inner = seg_len - KPRE + 1
    reach = (KPRE - 1) // 2

    def act_copy(g):
        return pltpu.make_async_copy(acts.at[g], act_ref.at[g], a_sem.at[g])

    def convolve(begin, end):
        @pl.loop(begin, end)
        def _(g):
            at = pl.ds(pl.multiple_of(g * GROUP, GROUP), GROUP)
            for q in range(KPRE):
                stacked[:, q * LANES : (q + 1) * LANES] = (
                    window[RIM + q : RIM + q + inner, at, :]
                    .reshape(inner * GROUP, LANES)
                    .astype(jnp.bfloat16)
                )
            extent = ext_out_ref[0, at, :]
            valid = jnp.concatenate(
                [hot(extent > t + reach + 0.5) for t in range(inner)], axis=0
            )
            valid = jnp.concatenate([valid] * (COL // LANES), axis=1)
            for c in range(0, bias_ref.shape[0], COL):
                cols = slice(c, c + COL)
                hidden = valid * (
                    f32_dot(stacked[...], w_pre[:, cols]) + bias_ref[cols].reshape(1, COL)
                )
                acts[g, :, cols] = snake(
                    hidden, snake_ref[0:1, cols], snake_ref[1:2, cols]
                ).astype(jnp.bfloat16)
            act_copy(g).start()

    groups_here = cap // GROUP
    cuts = (0, groups_here * 3 // 8, groups_here * 5 // 8, groups_here)
    load.wait()
    for tap_load in tap_loads:
        tap_load.start()
    convolve(cuts[0], cuts[1])
    home_pick = f32_dot(compact, select_t).astype(jnp.bfloat16)
    for copy in copies:
        copy.wait()

    arrived = got[...].astype(jnp.float32).reshape(rows, width + LANES)
    slot_of = arrived[:, width:]
    lane = lax.broadcasted_iota(jnp.int32, (rows, LANES), 1).astype(jnp.float32)
    place = hot(slot_of == lane + 1.0).astype(jnp.bfloat16)
    canon = lax.dot_general(
        place,
        arrived[:, :width].astype(jnp.bfloat16),
        (((0,), (0,)), ((), ())),
        preferred_element_type=jnp.float32,
    )[:slots].astype(jnp.bfloat16)
    head_tx[...] = canon[:, :half]
    tail_tx[...] = canon[:, half:]
    shift = [
        pltpu.make_async_remote_copy(
            src_ref=src, dst_ref=dst, send_sem=s2.at[k], recv_sem=r2.at[k],
            device_id=other, device_id_type=MESH,
        )
        for k, (src, dst, other) in enumerate(
            ((tail_tx, prev_rx, after_id), (head_tx, next_rx, before_id))
        )
    ]
    for copy in shift:
        copy.start()
    held = slot_of > 0.5
    low = slot_of - 1.0 - jnp.where(me == 0, 1.0, 0.0)
    low = jnp.where(low < -0.5, low + float(slots), low)
    high = slot_of - 1.0 + jnp.where(me == count - 1, 1.0, 0.0)
    high = jnp.where(high > slots - 0.5, high - float(slots), high)
    place_prev = hot((low == lane) & held).astype(jnp.bfloat16)[:, :slots]
    place_next = hot((high == lane) & held).astype(jnp.bfloat16)[:, :slots]
    convolve(cuts[1], cuts[2])
    for copy in shift:
        copy.wait()
    back[:, :, :half] = (
        f32_dot(place_prev, prev_rx[...]).reshape(workers, 8, half).astype(jnp.bfloat16)
    )
    back[:, :, half:] = (
        f32_dot(place_next, next_rx[...]).reshape(workers, 8, half).astype(jnp.bfloat16)
    )
    copies = swap(back, home, s3, r3)
    convolve(cuts[2], cuts[3])
    for copy in copies:
        copy.wait()
    homed = home[...].astype(jnp.float32).reshape(rows, width).astype(jnp.bfloat16)
    both = f32_dot(home_pick, homed)
    for t in range(RIM):
        window[t] = both[:, t * LANES : (t + 1) * LANES] * hot(ext[1] > t + seg_len - RIM + 0.5)
        window[RIM + seg_len + t] = both[:, half + t * LANES : half + (t + 1) * LANES] * hot(
            ext[2] > t + 0.5
        )
    span = seg_len + 2 * RIM
    for g in range(cap // GROUP):
        win_ref[g] = (
            window[:, g * GROUP : (g + 1) * GROUP, :]
            .reshape(span * GROUP, LANES)
            .astype(jnp.bfloat16)
        )
    for g in range(groups_here):
        act_copy(g).wait()
    for tap_load in tap_loads:
        tap_load.wait()


def exchange(mesh, features, target, extents, w_pre, biases, snake_params, w_up, up_bias):
    cap, seg_len, width = features.shape
    slots = cap // 2
    workers, groups = mesh.shape["voc"], mesh.shape["gen"]
    span = seg_len + 2 * RIM
    ch = w_pre.shape[1]
    inner = (seg_len - KPRE + 1) * GROUP
    hbm = pl.BlockSpec(memory_space=pl.ANY)
    vmem = pl.BlockSpec(memory_space=pltpu.VMEM)
    bf = jnp.bfloat16
    rim = RIM * width
    return pl.pallas_call(
        functools.partial(exchange_kernel, groups, workers, slots),
        out_shape=[
            jax.ShapeDtypeStruct((cap // GROUP, span * GROUP, width), bf),
            jax.ShapeDtypeStruct((3, cap, LANES), jnp.float32),
            jax.ShapeDtypeStruct((cap // GROUP, inner, ch), bf),
            jax.ShapeDtypeStruct(target.shape, jnp.int32),
            jax.ShapeDtypeStruct(biases.shape, jnp.float32),
            jax.ShapeDtypeStruct(snake_params.shape, jnp.float32),
            jax.ShapeDtypeStruct(up_bias.shape, jnp.float32),
            jax.ShapeDtypeStruct(w_pre.shape, bf),
            jax.ShapeDtypeStruct((2 * UP, ch, w_up.shape[1] // (2 * UP)), bf),
        ],
        in_specs=[pl.BlockSpec(memory_space=pltpu.HBM)] * 8,
        out_specs=[vmem] * 2 + [hbm] + [vmem] * 6,
        scratch_shapes=[
            pltpu.VMEM(features.shape, bf),
            pltpu.VMEM((3, cap), jnp.int32),
            pltpu.SemaphoreType.DMA((6,)),
            pltpu.VMEM((inner, KPRE * width), bf),
            pltpu.VMEM((cap // GROUP, inner, ch), bf),
            pltpu.VMEM((cap * seg_len, width), jnp.float32),
            pltpu.VMEM((span, cap, width), jnp.float32),
            pltpu.VMEM((workers, 8, 2 * rim + LANES), bf),
            pltpu.VMEM((workers, 8, 2 * rim + LANES), bf),
            pltpu.VMEM((slots, rim), bf),
            pltpu.VMEM((slots, rim), bf),
            pltpu.VMEM((slots, rim), bf),
            pltpu.VMEM((slots, rim), bf),
            pltpu.VMEM((workers, 8, 2 * rim), bf),
            pltpu.VMEM((workers, 8, 2 * rim), bf),
            pltpu.SemaphoreType.DMA((workers,)),
            pltpu.SemaphoreType.DMA((workers,)),
            pltpu.SemaphoreType.DMA((2,)),
            pltpu.SemaphoreType.DMA((2,)),
            pltpu.SemaphoreType.DMA((workers,)),
            pltpu.SemaphoreType.DMA((workers,)),
            pltpu.SemaphoreType.DMA,
            pltpu.SemaphoreType.DMA((2 * UP,)),
            pltpu.SemaphoreType.DMA((cap // GROUP,)),
        ],
        compiler_params=pltpu.CompilerParams(
            collective_id=0, has_side_effects=True, vmem_limit_bytes=14 * 2**20
        ),
        name="rim_exchange",
    )(
        *(
            pltpu.with_memory_space_constraint(value, pltpu.HBM)
            for value in (
                features, target, extents.T, biases, snake_params, up_bias, w_pre, w_up
            )
        )
    )


def vocode_kernel(
    target_ref, win_ref, ext_ref, w_pre_ref, bias_ref, snake_ref, up_bias_ref, taps, act_ref,
    out_ref,
    order, stacked, act_even, act_odd, wave32, wave16, zeros, z_sem, o_sem, a_sem,
):
    cap = target_ref.shape[0]
    span = win_ref.shape[1] // GROUP
    seg_len = span - 2 * RIM
    first = (KPRE - 1) // 2
    length = span - KPRE + 1
    ch = w_pre_ref.shape[1]
    ch2 = up_bias_ref.shape[0]
    samples = UP * seg_len
    col = COL
    inner = act_ref.shape[1]
    edge = RIM * GROUP

    def centre_tap(r):
        return r + UP // 2

    def side_tap(r):
        return r + 3 * UP // 2 if r < UP // 2 else r - UP // 2

    def act_load(g):
        return pltpu.make_async_copy(
            act_ref.at[g], act_even.at[g, pl.ds(edge, inner)], a_sem.at[g]
        )

    act_load(0).start()
    act_load(1).start()
    def place(i, state):
        a, b = state
        live = jnp.where(target_ref[i] >= 0, 1, 0)
        order[jnp.where(live == 1, a, b)] = i
        return a + live, b - 1 + live

    used, _ = lax.fori_loop(0, cap, place, (0, cap - 1), unroll=True)
    n_groups = lax.div(used + GROUP - 1, GROUP)

    @pl.loop(2, cap // GROUP)
    def _(g):
        act_load(g).start()

    zeros[...] = jnp.zeros_like(zeros)

    def zero_copy(i):
        return pltpu.make_async_copy(zeros, out_ref.at[order[i]], z_sem.at[i])

    @pl.loop(n_groups * GROUP, cap)
    def _(i):
        zero_copy(i).start()

    def frame_mask(g, t):
        at = pl.ds(pl.multiple_of(g * GROUP, GROUP), GROUP)
        if t < RIM:
            return hot(ext_ref[1, at, :] > t + seg_len - RIM + 0.5)
        if t < RIM + seg_len:
            return hot(ext_ref[0, at, :] > t - RIM + 0.5)
        return hot(ext_ref[2, at, :] > t - RIM - seg_len + 0.5)

    @pl.loop(0, n_groups)
    def _(g):
        frames = win_ref[g].astype(jnp.float32)
        last = (length - RIM) * GROUP
        for q in range(KPRE):
            lanes = slice(q * LANES, (q + 1) * LANES)
            low = frames[q * GROUP : q * GROUP + edge]
            high = frames[last + q * GROUP : last + q * GROUP + edge]
            stacked[:, lanes] = jnp.concatenate([low, high], axis=0).astype(jnp.bfloat16)
        outer = list(range(RIM)) + list(range(length - RIM, length))
        valid = jnp.concatenate([frame_mask(g, first + t) for t in outer], axis=0)
        valid = jnp.concatenate([valid] * (col // LANES), axis=1)
        act_load(g).wait()
        for c in range(0, ch, col):
            cols = slice(c, c + col)
            hidden = valid * (
                f32_dot(stacked[...], w_pre_ref[:, cols]) + bias_ref[cols].reshape(1, col)
            )
            act = snake(hidden, snake_ref[0:1, cols], snake_ref[1:2, cols])
            act_even[g, :edge, cols] = act[:edge].astype(jnp.bfloat16)
            act_even[g, edge + inner :, cols] = act[edge:].astype(jnp.bfloat16)
            middle = act_even[g, edge : edge + inner, cols].astype(jnp.float32)
            act_odd[g, :, cols] = jnp.concatenate(
                [act[GROUP:edge], middle, act[edge : 2 * edge - GROUP]], axis=0
            ).astype(jnp.bfloat16)

    @pl.loop(n_groups, cap // GROUP)
    def _(g):
        act_load(g).wait()

    def wave_copy(g, slot, k):
        return pltpu.make_async_copy(
            wave16.at[slot, k], out_ref.at[order[g * GROUP + k]], o_sem.at[slot, k]
        )

    rows = seg_len * GROUP
    pitch = samples + 1

    @pl.loop(0, n_groups)
    def _(g):
        slot = lax.rem(g, 2)

        @pl.when(g >= 2)
        def _():
            for k in range(GROUP):
                wave_copy(g - 2, slot, k).wait()

        for c in range(0, ch2, col):
            cols = slice(c, c + col)
            bias = up_bias_ref[cols].reshape(1, col)
            for r in range(UP):
                side_at = 0 if r < UP // 2 else 2 * GROUP
                total = f32_dot(act_odd[g], taps[centre_tap(r), :, cols]) + f32_dot(
                    act_even[g, side_at : side_at + rows, :], taps[side_tap(r), :, cols]
                )
                total = total + bias
                for j in range(seg_len):
                    keep = frame_mask(g, RIM + j)
                    for h in range(col // LANES):
                        block = (c // LANES + h) * GROUP
                        wave32[pl.ds(block * pitch + UP * j + r, GROUP, stride=pitch), :] = (
                            keep * total[j * GROUP : (j + 1) * GROUP, h * LANES : (h + 1) * LANES]
                        )
            for h in range(c // LANES, (c + col) // LANES):
                for k in range(GROUP):
                    start = (h * GROUP + k) * pitch
                    wave16[slot, k, :, h * LANES : (h + 1) * LANES] = wave32[
                        start : start + samples, :
                    ].astype(jnp.bfloat16)

        for k in range(GROUP):
            wave_copy(g, slot, k).start()

    for lag in (2, 1):

        @pl.when(n_groups >= lag)
        def _():
            g = n_groups - lag
            for k in range(GROUP):
                wave_copy(g, lax.rem(g, 2), k).wait()

    @pl.loop(n_groups * GROUP, cap)
    def _(i):
        zero_copy(i).wait()


def vocode(target, window, ext, acts, w_pre, biases, snake_params, taps, up_bias):
    cap, width = target.shape[0], window.shape[2]
    span = window.shape[1] // GROUP
    seg_len = span - 2 * RIM
    ch, ch2 = w_pre.shape[1], up_bias.shape[0]
    length = span - KPRE + 1
    groups = cap // GROUP
    samples = UP * seg_len
    vmem = pl.BlockSpec(memory_space=pltpu.VMEM)
    hbm = pl.BlockSpec(memory_space=pl.ANY)
    rows = cap * seg_len
    return pl.pallas_call(
        vocode_kernel,
        out_shape=jax.ShapeDtypeStruct((cap, samples, ch2), jnp.bfloat16),
        in_specs=[pl.BlockSpec(memory_space=pltpu.SMEM)] + [vmem] * 7 + [hbm],
        out_specs=hbm,
        scratch_shapes=[
            pltpu.SMEM((cap,), jnp.int32),
            pltpu.VMEM((2 * RIM * GROUP, KPRE * width), jnp.bfloat16),
            pltpu.VMEM((groups, length * GROUP, ch), jnp.bfloat16),
            pltpu.VMEM((groups, seg_len * GROUP, ch), jnp.bfloat16),
            pltpu.VMEM((ch2 // LANES * GROUP * (samples + 1), LANES), jnp.float32),
            pltpu.VMEM((2, GROUP, samples, ch2), jnp.bfloat16),
            pltpu.VMEM((samples, ch2), jnp.bfloat16),
            pltpu.SemaphoreType.DMA((cap,)),
            pltpu.SemaphoreType.DMA((2, GROUP)),
            pltpu.SemaphoreType.DMA((groups,)),
        ],
        compiler_params=pltpu.CompilerParams(vmem_limit_bytes=22 * 2**20),
        cost_estimate=pl.CostEstimate(
            flops=2 * rows * ch * (KPRE * width + 2 * UP * ch2),
            bytes_accessed=2 * (w_pre.size + taps.size + rows * UP * ch2),
            transcendentals=0,
        ),
        name="vocode_used",
    )(target, window, ext, w_pre, biases, snake_params, up_bias, taps, acts)


def solution(mesh):
    def on_device(features, target, extents, w_pre, biases, snake_params, w_up, up_bias):
        window, ext, acts, target, biases, snake_params, up_bias, w_near, taps = exchange(
            mesh, features, target, extents, w_pre, biases, snake_params, w_up, up_bias
        )
        return vocode(target, window, ext, acts, w_near, biases, snake_params, taps, up_bias)

    placed = (
        P(("gen", "voc"), None, None),
        P(("gen", "voc")),
        P(("gen", "voc"), None),
        P(),
        P(),
        P(),
        P(),
        P(),
    )
    return jax.shard_map(
        on_device,
        mesh=mesh,
        in_specs=placed,
        out_specs=P(("gen", "voc"), None, None),
        check_vma=False,
    )
```
